512 devices in a mesh: dp: 4 (over z_hi), segment: 16 (over y, core), patch: 8 (over x, z_lo).
Axes of the slice: x: 4, y: 8, z: 8 (z_hi: 4, z_lo: 2; z = z_hi * 2 + z_lo), core: 2. Of those that a mesh axis runs over, the one named last changes fastest.
Arguments:
- hidden: bfloat16 [64, 1024, 1536], P(('dp', 'segment'), 'patch'), parts along dimension 0, may hold values from -6 to 6
- w_qkv: bfloat16 [16, 1536, 4608], P('segment', None, 'patch'), may hold values from -0.12552947 to 0.12552947
- norm_gain: float32 [16, 1536], P('segment'), may hold values from 0.5 to 1.5
- box_vec: float32 [16, 1536], P('segment'), may hold values from -4 to 4
- gate: float32 [64, 1536], P(('dp', 'segment')), parts along dimension 0, may hold values from 4 to 16
- box_mask: int32 [64, 1024], P(('dp', 'segment'), 'patch'), parts along dimension 0, may hold values 0 or 1
- stale_kv: bfloat16 [64, 2, 1024, 1536], P(('dp', 'segment'), None, 'patch'), parts along dimension 0, may hold values from -6 to 6
Outputs:
- hidden_out: bfloat16 [64, 1024, 1536], P(('dp', 'segment'), 'patch'), parts along dimension 0
- fresh_kv: bfloat16 [64, 2, 1024, 1536], P(('dp', 'segment'), None, 'patch'), parts along dimension 0
The draws below stay inside these ranges and needn't reach their ends.
There are 4 independent parts, one for each index of `dp`. The reference program is written for one: setup_inputs(seed, part) draws one part's arguments, and reference() takes and returns one part's arrays. A program takes and returns all parts, laid end to end along the dimension named above; an argument that names none is the same for every part. Nothing has to cross between parts.
All inputs are finite; a program needn't handle non-finite values. No bound on the sum of `box_mask` on one device may be relied on, other than what follows from the above.
Results may differ from the reference program's by a relative error of at most 0.023.
Values may be sent and summed in bfloat16 or wider, within the bound.
No kernel may reach another device: no remote copies, remote signals or barrier semaphores. Data moves between devices by JAX's collectives and lax.ppermute only.
A program may use at most 64 MiB of HBM per device.

```python
import jax
import jax.numpy as jnp
from jax import lax

D = 1536
HEADS = 12
HEAD_DIM = 128
ROWS = 128
HW = 1536
TOKENS = 1024
LAYERS = 16
N_PATCH = 8


def box_rows(key):
    drawn = jax.random.normal(jax.random.fold_in(key, 101), (LAYERS, D), jnp.float32)
    return jnp.clip(drawn, -4.0, 4.0)


def draw_box_vec(key, part):
    return box_rows(key)


def draw_w_qkv(key, part):
    drawn = jax.random.normal(jax.random.fold_in(key, 102), (LAYERS, D, 3 * HW), jnp.float32)
    base = jnp.clip(drawn, -4.0, 4.0) * D ** (-0.5)
    return base.astype(jnp.bfloat16)


def with_ends(entries, rng, low, high):
    longest = entries.shape.index(max(entries.shape))
    spots = []
    for shift in (0, 1):
        where = [jax.random.randint(jax.random.fold_in(rng, axis), (), 0, length) for axis, length in enumerate(entries.shape)]
        where[longest] = (where[longest] + shift) % entries.shape[longest]
        spots.append(tuple(where))
    return entries.at[spots[0]].set(low).at[spots[1]].set(high)


def block_scale(key, shape, pieces, smallest, top_value):
    loudness = 1.0
    for dim, parts in pieces:
        steps = jax.random.uniform(jax.random.fold_in(jax.random.fold_in(key, 6), dim), (parts,), jnp.float32, smallest / len(pieces), top_value / len(pieces))
        loudness = loudness * jnp.repeat(jnp.exp(steps), shape[dim] // parts).reshape((-1,) + (1,) * (len(shape) - 1 - dim))
    return loudness


def scatter_about(stream_key, shape, scale, most, shards=(), kind=jnp.bfloat16):
    values = jax.random.normal(stream_key, shape, jnp.float32) * scale
    if len(shards) > 0:
        values = block_scale(stream_key, shape, shards, -0.22, 0.18) * values
    return jnp.clip(values, min=-most, max=most).astype(kind)


def setup_inputs(seed: int = 0, part: int = 0) -> dict:
    splits = jax.random.split(jax.random.key(seed), 8)
    part_splits = jax.random.split(jax.random.fold_in(splits[7], part), 8)
    hidden = scatter_about(part_splits[0], (LAYERS, TOKENS, D), 1.0, 6.0, ((0, 16), (1, 8)))
    w_qkv = draw_w_qkv(jax.random.fold_in(splits[7], 71), part)
    norm_gain = jnp.clip(1.0 + 0.1 * jax.random.normal(splits[2], (LAYERS, D), jnp.float32), 0.5, 1.5)
    box_vec = draw_box_vec(jax.random.fold_in(splits[7], 71), part)
    gate = jnp.clip(4.0 + 12.0 * jax.random.uniform(part_splits[4], (LAYERS, D), jnp.float32) ** block_scale(part_splits[4], (LAYERS, D), ((0, 16),), -0.2, 0.2), 4.0, 16.0)
    box_mask = with_ends((jax.random.randint(part_splits[5], (LAYERS, TOKENS), 0, 2) < 1).astype(jnp.int32), jax.random.fold_in(part_splits[5], 1), 0, 1)
    stale_kv = scatter_about(part_splits[6], (LAYERS, 2, TOKENS, HW), 1.0, 6.0, ((0, 16), (2, 8)))
    return {"hidden": hidden, "w_qkv": w_qkv, "norm_gain": norm_gain, "box_vec": box_vec, "gate": gate, "box_mask": box_mask, "stale_kv": stale_kv}


def attend(queries, keys, values):
    count = queries.shape[0]
    length = keys.shape[0]
    qh = queries.astype(jnp.float32).reshape(count, HEADS, HEAD_DIM)
    kh = keys.astype(jnp.float32).reshape(length, HEADS, HEAD_DIM)
    vh = values.astype(jnp.float32).reshape(length, HEADS, HEAD_DIM)
    scores = jnp.einsum('nhd,thd->nht', qh, kh) * HEAD_DIM ** (-0.5)
    top = lax.optimization_barrier(jnp.max(scores, axis=-1))
    weights = jnp.exp(scores - top[..., None])
    total = lax.optimization_barrier(jnp.sum(weights, axis=-1))
    rounded = weights.astype(jnp.bfloat16).astype(jnp.float32)
    summed = jnp.einsum('nht,thd->nhd', rounded, vh)
    return (summed / total[..., None]).reshape(count, HEADS * HEAD_DIM)

def one_layer(packed):
    state, weight, gain, boxv, gates, mask, stale = packed
    hf = state.astype(jnp.float32)
    inverse = lax.rsqrt(lax.optimization_barrier(jnp.mean(hf * hf, axis=-1, keepdims=True)) + 1e-06)
    normed = (hf * inverse * gain + mask[:, None].astype(jnp.float32) * boxv).astype(jnp.bfloat16)
    qkv = jnp.dot(normed, weight, preferred_element_type=jnp.float32).astype(jnp.bfloat16)
    width = HEADS * HEAD_DIM
    queries = qkv[:, :width]
    keys_new = qkv[:, width:2 * width]
    values_new = qkv[:, 2 * width:]

    def per_patch(index):
        start = (index * ROWS).astype(jnp.int32)
        block_q = lax.dynamic_slice_in_dim(queries, start, ROWS, 0)
        keys = lax.dynamic_update_slice_in_dim(stale[0], lax.dynamic_slice_in_dim(keys_new, start, ROWS, 0), start, 0)
        values = lax.dynamic_update_slice_in_dim(stale[1], lax.dynamic_slice_in_dim(values_new, start, ROWS, 0), start, 0)
        return attend(block_q, keys, values)
    attended = lax.map(per_patch, jnp.arange(N_PATCH, dtype=jnp.int32)).reshape(TOKENS, width)
    updated = (hf + gates * attended).astype(jnp.bfloat16)
    return (updated, jnp.stack([keys_new, values_new]))

def reference(hidden, w_qkv, norm_gain, box_vec, gate, box_mask, stale_kv):
    updated, fresh = lax.map(one_layer, (hidden, w_qkv, norm_gain, box_vec, gate, box_mask, stale_kv))
    return (jnp.roll(updated, 1, axis=0), fresh)
```

```python
import jax
import jax.numpy as jnp
from jax import lax
from jax.experimental import pallas as pl
from jax.experimental.pallas import tpu as pltpu
from jax.sharding import PartitionSpec as P

HEAD_DIM = 128
ROWS = 128
D = 1536
UNIT = 384
HALF = 192
SCALE = HEAD_DIM ** (-0.5)
BF = jnp.bfloat16
F32 = jnp.float32
NT = (((1,), (1,)), ((), ()))
VM = pl.BlockSpec(memory_space=pltpu.VMEM)
PARAMS = pltpu.CompilerParams(vmem_limit_bytes=48 * 1024 * 1024)


def spot(x, z):
    return 2 * (x % 4) + z


def ahead(z):
    return 1 - 2 * z


def x_pairs(steps):
    return [(spot(x, z), spot(x + ahead(z) * steps, z)) for x in range(4) for z in range(2)]


def partner_pairs():
    return [(spot(x, z), spot(x, 1 - z)) for x in range(4) for z in range(2)]


def far_pairs(parts):
    pairs = []
    for dp in range(parts):
        for x in range(4):
            for z in range(2):
                there = (2 * dp + z - ahead(z)) % (2 * parts)
                pairs.append((dp * 8 + spot(x, z), (there // 2) * 8 + spot(x, there % 2)))
    return pairs


def where_am_i():
    p = lax.axis_index("patch")
    return p // 2, p % 2


def call(body, out, count, **more):
    return pl.pallas_call(
        body,
        out_shape=out,
        in_specs=[VM] * count,
        out_specs=jax.tree.map(lambda _: VM, out),
        compiler_params=PARAMS,
        **more,
    )


def norm_body(h_ref, g_ref, b_ref, m_ref, o_ref):
    h = h_ref[0].astype(F32)
    inverse = lax.rsqrt(jnp.mean(h * h, axis=-1, keepdims=True) + 1e-06)
    mask = jnp.broadcast_to(m_ref[...].astype(F32), (ROWS, ROWS)).T[:, :1]
    o_ref[...] = (h * inverse * g_ref[...] + mask * b_ref[...]).astype(BF)


def project(blocks, weight, o_ref):
    x, z = where_am_i()
    tokens = jnp.concatenate([b[...] for b in blocks], axis=0)
    got = lax.dot_general(tokens, weight, NT, preferred_element_type=F32).astype(BF)
    for j in range(4):
        o_ref[(x + (1 - 2 * z) * j + 4) % 4] = got[ROWS * j : ROWS * (j + 1)]


def front_body(t0, t1, t2, t3, w_ref, o_ref):
    _, z = where_am_i()
    project((t0, t1, t2, t3), w_ref[pl.ds(pl.multiple_of(HALF * z, HALF), UNIT), :], o_ref)


def back_body(t0, t1, t2, t3, w_ref, o_ref):
    project((t0, t1, t2, t3), w_ref[...], o_ref)


def mid_body(t0, t1, t2, t3, w_ref, u_ref, o_ref, both):
    _, z = where_am_i()
    mine = w_ref[pl.ds(pl.multiple_of(UNIT * (1 - z), HALF), HALF), :]
    both[pl.ds(pl.multiple_of(HALF * z, HALF), HALF), :] = mine
    both[pl.ds(pl.multiple_of(HALF * (1 - z), HALF), HALF), :] = u_ref[...]
    project((t0, t1, t2, t3), both[...], o_ref)


def pick(index, refs, at):
    a, b, c = (r[at] for r in refs)
    return jnp.where(index == 0, a, jnp.where(index == 1, b, c))


def roles(x, z):
    left = 1 + z
    right = 2 - z
    q = jnp.where(x == 0, 0, jnp.where(x == 3, right, left))
    k = jnp.where(x == 0, right, jnp.where(x == 3, left, 0))
    v = jnp.where(x == 0, left, jnp.where(x == 3, 0, right))
    return q, k, v


def attend_body(a_ref, b_ref, c_ref, s_ref, o_ref):
    x, z = where_am_i()
    refs = (a_ref, b_ref, c_ref)
    qi, ki, vi = roles(x, z)
    for j in range(4):
        o_ref[j, 1] = pick(ki, refs, j)
        o_ref[j, 2] = pick(vi, refs, j)
    for head in range(3):
        cols = slice(HEAD_DIM * head, HEAD_DIM * (head + 1))
        kept = [
            [s_ref[2 * j + side, kv, :, cols] for side in (z, 1 - z) for j in range(4)]
            for kv in range(2)
        ]
        for j in range(4):
            q = pick(qi, refs, (j, slice(None), cols))
            keys = list(kept[0])
            values = list(kept[1])
            keys[j] = o_ref[j, 1, :, cols]
            values[j] = o_ref[j, 2, :, cols]
            scores = lax.dot_general(
                q, jnp.concatenate(keys, axis=0), NT, preferred_element_type=F32
            ) * SCALE
            top = jnp.max(scores, axis=-1, keepdims=True)
            weights = jnp.exp(scores - top)
            total = jnp.sum(weights, axis=-1, keepdims=True)
            summed = jnp.dot(
                weights.astype(BF), jnp.concatenate(values, axis=0), preferred_element_type=F32
            )
            o_ref[j, 0, :, cols] = (summed / total).astype(BF)


def finish_body(r_ref, h_ref, g_ref, o_ref, f_ref):
    for group in range(4):
        cols = slice(UNIT * group, UNIT * (group + 1))
        r = r_ref.at[group ^ 1]
        o_ref[0, :, cols] = (
            h_ref[0, :, cols].astype(F32) + g_ref[:, cols] * r[0].astype(F32)
        ).astype(BF)
        f_ref[0, 0, :, cols] = r[1]
        f_ref[0, 1, :, cols] = r[2]


def local(hidden, w_qkv, norm_gain, box_vec, gate, box_mask, stale_kv):
    parts = lax.axis_size("dp")
    segments = lax.axis_size("segment")
    _, z = where_am_i()
    shape = jax.ShapeDtypeStruct
    unit = shape((4, ROWS, UNIT), BF)

    normed = call(norm_body, shape((ROWS, D), BF), 4)(hidden, norm_gain, box_vec, box_mask)
    weight = jnp.swapaxes(w_qkv[0], 0, 1)
    lead = lax.dynamic_slice_in_dim(weight, HALF * z, UNIT, 0)
    rest = lax.dynamic_slice_in_dim(weight, UNIT * (1 - z), HALF, 0)
    lead = lax.ppermute(lead, ("dp", "patch"), far_pairs(parts))
    rest = lax.ppermute(rest, "patch", partner_pairs())
    t1 = lax.ppermute(normed, "patch", x_pairs(3))
    t3 = lax.ppermute(normed, "patch", x_pairs(1))
    t2 = lax.ppermute(normed, "patch", x_pairs(2))
    tokens = (normed, t1, t2, t3)

    groups = [stale_kv[0, :, :, UNIT * (p // 2 ^ 1) : UNIT * (p // 2 ^ 1) + UNIT] for p in range(8)]
    kept = lax.all_to_all(jnp.stack(groups), "patch", 0, 0)

    front = call(front_body, unit, 5)(*tokens, weight)
    front = lax.ppermute(front, "patch", x_pairs(1))
    back = call(back_body, unit, 5)(*tokens, lead)
    back = lax.ppermute(back, "patch", x_pairs(3))
    mid = call(mid_body, unit, 6, scratch_shapes=[pltpu.VMEM((UNIT, D), BF)])(*tokens, weight, rest)

    mixed = call(attend_body, shape((4, 3, ROWS, UNIT), BF), 4)(mid, front, back, kept)
    mixed = lax.all_to_all(
        mixed, "patch", 0, 0, axis_index_groups=[[0, 2, 4, 6], [1, 3, 5, 7]]
    )
    updated, fresh = call(
        finish_body, (shape((1, ROWS, D), BF), shape((1, 2, ROWS, D), BF)), 3
    )(mixed, hidden, gate)
    passed = lax.ppermute(updated, "segment", [(i, (i + 1) % segments) for i in range(segments)])
    return (passed, fresh)


def solution(mesh):
    placed = (
        P(("dp", "segment"), "patch", None),
        P("segment", None, "patch"),
        P("segment", None),
        P("segment", None),
        P(("dp", "segment"), None),
        P(("dp", "segment"), "patch"),
        P(("dp", "segment"), None, "patch", None),
    )
    return jax.shard_map(
        local,
        mesh=mesh,
        in_specs=placed,
        out_specs=(P(("dp", "segment"), "patch", None), P(("dp", "segment"), None, "patch", None)),
        check_vma=False,
    )
```

```python
import jax
import jax.numpy as jnp
from jax import lax
from jax.experimental import pallas as pl
from jax.experimental.pallas import tpu as pltpu
from jax.sharding import PartitionSpec as P

HEAD_DIM = 128
ROWS = 128
D = 1536
UNIT = 384
HALF = 192
SCALE = HEAD_DIM ** (-0.5)
BF = jnp.bfloat16
F32 = jnp.float32
NT = (((1,), (1,)), ((), ()))
VM = pl.BlockSpec(memory_space=pltpu.VMEM)
PARAMS = pltpu.CompilerParams(vmem_limit_bytes=16 * 1024 * 1024)


def spot(x, z):
    return 2 * (x % 4) + z


def ahead(z):
    return 1 - 2 * z


def x_pairs(steps):
    return [(spot(x, z), spot(x + ahead(z) * steps, z)) for x in range(4) for z in range(2)]


def partner_pairs():
    return [(spot(x, z), spot(x, 1 - z)) for x in range(4) for z in range(2)]


def far_pairs(parts):
    pairs = []
    for dp in range(parts):
        for x in range(4):
            for z in range(2):
                there = (2 * dp + z - ahead(z)) % (2 * parts)
                pairs.append((dp * 8 + spot(x, z), (there // 2) * 8 + spot(x, there % 2)))
    return pairs


def where_am_i():
    p = lax.axis_index("patch")
    return p // 2, p % 2


def call(body, out, count, **more):
    return pl.pallas_call(
        body,
        out_shape=out,
        in_specs=[VM] * count,
        out_specs=jax.tree.map(lambda _: VM, out),
        compiler_params=PARAMS,
        **more,
    )


def norm_body(h_ref, g_ref, b_ref, m_ref, o_ref):
    h = h_ref[0].astype(F32)
    inverse = lax.rsqrt(jnp.mean(h * h, axis=-1, keepdims=True) + 1e-06)
    mask = jnp.broadcast_to(m_ref[...].astype(F32), (ROWS, ROWS)).T[:, :1]
    o_ref[...] = (h * inverse * g_ref[...] + mask * b_ref[...]).astype(BF)


def spread_body(s_ref, n_ref, o_ref):
    del n_ref
    for x in range(4):
        for z in range(2):
            o_ref[spot(x, z)] = s_ref[0, :, :, UNIT * (x ^ 1) : UNIT * ((x ^ 1) + 1)]


def project(blocks, weight, o_ref):
    x, z = where_am_i()
    tokens = jnp.concatenate([b[...] for b in blocks], axis=0)
    got = lax.dot_general(tokens, weight, NT, preferred_element_type=F32).astype(BF)
    for j in range(4):
        o_ref[(x + (1 - 2 * z) * j + 4) % 4] = got[ROWS * j : ROWS * (j + 1)]


def front_body(t0, t1, t2, t3, w_ref, early_ref, o_ref):
    del early_ref
    _, z = where_am_i()
    project((t0, t1, t2, t3), w_ref[pl.ds(pl.multiple_of(HALF * z, HALF), UNIT), :], o_ref)


def back_body(t0, t1, t2, t3, w_ref, o_ref):
    project((t0, t1, t2, t3), w_ref[...], o_ref)


def mid_body(t0, t1, t2, t3, w_ref, u_ref, o_ref, both):
    _, z = where_am_i()
    mine = w_ref[pl.ds(pl.multiple_of(UNIT * (1 - z), HALF), HALF), :]
    both[pl.ds(pl.multiple_of(HALF * z, HALF), HALF), :] = mine
    both[pl.ds(pl.multiple_of(HALF * (1 - z), HALF), HALF), :] = u_ref[...]
    project((t0, t1, t2, t3), both[...], o_ref)


def pick(index, refs, at):
    a, b, c = (r[at] for r in refs)
    return jnp.where(index == 0, a, jnp.where(index == 1, b, c))


def roles(x, z):
    left = 1 + z
    right = 2 - z
    q = jnp.where(x == 0, 0, jnp.where(x == 3, right, left))
    k = jnp.where(x == 0, right, jnp.where(x == 3, left, 0))
    v = jnp.where(x == 0, left, jnp.where(x == 3, 0, right))
    return q, k, v


def sort_body(a_ref, b_ref, c_ref, q_ref, kv_ref):
    refs = (a_ref, b_ref, c_ref)
    qi, ki, vi = roles(*where_am_i())
    for j in range(4):
        q_ref[j] = pick(qi, refs, j)
        kv_ref[j, 0] = pick(ki, refs, j)
        kv_ref[j, 1] = pick(vi, refs, j)


def attend_body(q_ref, kv_ref, s_ref, g_ref, *o_refs):
    x, z = where_am_i()
    gates = g_ref[x ^ 1]
    for head in range(3):
        cols = slice(HEAD_DIM * head, HEAD_DIM * (head + 1))
        kept = [
            [s_ref[2 * j + side, kv, :, cols] for side in (z, 1 - z) for j in range(4)]
            for kv in range(2)
        ]
        for j in range(4):
            q = q_ref[j, :, cols]
            keys = list(kept[0])
            values = list(kept[1])
            keys[j] = kv_ref[j, 0, :, cols]
            values[j] = kv_ref[j, 1, :, cols]
            scores = lax.dot_general(
                q, jnp.concatenate(keys, axis=0), NT, preferred_element_type=F32
            ) * SCALE
            top = jnp.max(scores, axis=-1, keepdims=True)
            weights = jnp.exp(scores - top)
            total = jnp.sum(weights, axis=-1, keepdims=True)
            summed = jnp.dot(
                weights.astype(BF), jnp.concatenate(values, axis=0), preferred_element_type=F32
            )
            o_refs[0][j, :, cols] = (gates[:, cols] * (summed / total)).astype(BF)


def finish_body(a0, a1, a2, a3, h_ref, o_ref):
    x, z = where_am_i()
    for j, ref in enumerate((a0, a1, a2, a3)):
        group = ((x + (1 - 2 * z) * j + 4) % 4) ^ 1
        cols = pl.ds(pl.multiple_of(UNIT * group, UNIT), UNIT)
        o_ref[0, :, cols] = (h_ref[0, :, cols].astype(F32) + ref[...].astype(F32)).astype(BF)


def fresh_body(r_ref, f_ref):
    for group in range(4):
        f_ref[0, :, :, UNIT * group : UNIT * (group + 1)] = r_ref[group ^ 1]


def local(hidden, w_qkv, norm_gain, box_vec, gate, box_mask, stale_kv):
    parts = lax.axis_size("dp")
    segments = lax.axis_size("segment")
    _, z = where_am_i()
    shape = jax.ShapeDtypeStruct
    unit = shape((4, ROWS, UNIT), BF)

    normed = call(norm_body, shape((ROWS, D), BF), 4)(hidden, norm_gain, box_vec, box_mask)
    weight = jnp.swapaxes(w_qkv[0], 0, 1)
    lead = lax.dynamic_slice_in_dim(weight, HALF * z, UNIT, 0)
    rest = lax.dynamic_slice_in_dim(weight, UNIT * (1 - z), HALF, 0)
    lead = lax.ppermute(lead, ("dp", "patch"), far_pairs(parts))
    rest = lax.ppermute(rest, "patch", partner_pairs())
    t1 = lax.ppermute(normed, "patch", x_pairs(3))
    t3 = lax.ppermute(normed, "patch", x_pairs(1))
    t2 = lax.ppermute(normed, "patch", x_pairs(2))
    tokens = (normed, t1, t2, t3)

    spread = call(spread_body, shape((8, 2, ROWS, UNIT), BF), 2)(stale_kv, t1)
    kept = lax.all_to_all(spread, "patch", 0, 0)

    before = lax.ppermute(hidden, "segment", [(i, (i + 1) % segments) for i in range(segments)])
    front = call(front_body, unit, 6)(*tokens, weight, before)
    front = lax.ppermute(front, "patch", x_pairs(1))
    back = call(back_body, unit, 5)(*tokens, lead)
    back = lax.ppermute(back, "patch", x_pairs(3))
    mid = call(mid_body, unit, 6, scratch_shapes=[pltpu.VMEM((UNIT, D), BF)])(*tokens, weight, rest)

    queries, own_kv = call(sort_body, (unit, shape((4, 2, ROWS, UNIT), BF)), 3)(mid, front, back)
    fresh = lax.all_to_all(
        own_kv, "patch", 0, 0, axis_index_groups=[[0, 2, 4, 6], [1, 3, 5, 7]]
    )
    fresh = call(fresh_body, shape((1, 2, ROWS, D), BF), 1)(fresh)
    mixed = call(attend_body, (unit,), 4)(queries, own_kv, kept, gate.reshape(4, 1, UNIT))[0]

    x, _ = where_am_i()
    came = []
    for j in range(4):
        there = lax.rem(x + (1 - 2 * z) * j + 4, 4)
        piece = lax.dynamic_index_in_dim(mixed, there, 0, keepdims=False)
        pairs = [
            (s * 8 + src, (s + 1) % segments * 8 + dst)
            for s in range(segments)
            for src, dst in x_pairs(j)
        ]
        came.append(lax.ppermute(piece, ("segment", "patch"), pairs))
    passed = call(finish_body, shape((1, ROWS, D), BF), 5)(
        came[0], came[3], came[2], came[1], before
    )
    return (passed, fresh)


def solution(mesh):
    placed = (
        P(("dp", "segment"), "patch", None),
        P("segment", None, "patch"),
        P("segment", None),
        P("segment", None),
        P(("dp", "segment"), None),
        P(("dp", "segment"), "patch"),
        P(("dp", "segment"), None, "patch", None),
    )
    return jax.shard_map(
        local,
        mesh=mesh,
        in_specs=placed,
        out_specs=(P(("dp", "segment"), "patch", None), P(("dp", "segment"), None, "patch", None)),
        check_vma=False,
    )
```

```python
import jax
import jax.numpy as jnp
from jax import lax
from jax.experimental import pallas as pl
from jax.experimental.pallas import tpu as pltpu
from jax.sharding import PartitionSpec as P

HEAD_DIM = 128
ROWS = 128
D = 1536
UNIT = 384
HALF = 192
SCALE = HEAD_DIM ** (-0.5)
BF = jnp.bfloat16
F32 = jnp.float32
NT = (((1,), (1,)), ((), ()))
VM = pl.BlockSpec(memory_space=pltpu.VMEM)
PARAMS = pltpu.CompilerParams(vmem_limit_bytes=16 * 1024 * 1024)


def spot(x, z):
    return 2 * (x % 4) + z


def ahead(z):
    return 1 - 2 * z


def x_pairs(steps):
    return [(spot(x, z), spot(x + ahead(z) * steps, z)) for x in range(4) for z in range(2)]


def partner_pairs():
    return [(spot(x, z), spot(x, 1 - z)) for x in range(4) for z in range(2)]


def far_pairs(parts):
    pairs = []
    for dp in range(parts):
        for x in range(4):
            for z in range(2):
                there = (2 * dp + z - ahead(z)) % (2 * parts)
                pairs.append((dp * 8 + spot(x, z), (there // 2) * 8 + spot(x, there % 2)))
    return pairs


def where_am_i():
    p = lax.axis_index("patch")
    return p // 2, p % 2


def call(body, out, count, **more):
    return pl.pallas_call(
        body,
        out_shape=out,
        in_specs=[VM] * count,
        out_specs=jax.tree.map(lambda _: VM, out),
        compiler_params=PARAMS,
        **more,
    )


def norm_body(h_ref, g_ref, b_ref, m_ref, s_ref, w_ref, own, b1, b2, b3, lead, rest):
    x, z = where_am_i()
    h = h_ref[0].astype(F32)
    inverse = lax.rsqrt(jnp.mean(h * h, axis=-1, keepdims=True) + 1e-06)
    mask = jnp.broadcast_to(m_ref[...].astype(F32), (ROWS, ROWS)).T[:, :1]
    normed = (h * inverse * g_ref[...] + mask * b_ref[...]).astype(BF)
    for j, bundle in enumerate((own, b1, b2, b3)):
        for g in range(4):
            bundle[g] = normed[:, UNIT * g : UNIT * (g + 1)]
        group = ((x + (1 - 2 * z) * j + 4) % 4) ^ 1
        cols = pl.ds(pl.multiple_of(UNIT * group, UNIT), UNIT)
        bundle[4] = s_ref[0, 0, :, cols]
        bundle[5] = s_ref[0, 1, :, cols]
    lead[...] = w_ref[pl.ds(pl.multiple_of(HALF * z, HALF), UNIT), :]
    rest[...] = w_ref[pl.ds(pl.multiple_of(UNIT * (1 - z), HALF), HALF), :]


def near_body(t0, t1, t3, o_ref):
    for i, ref in enumerate((t0, t1, t3)):
        o_ref[i] = ref[4:6]


def far_body(t2, o_ref):
    o_ref[...] = t2[4:6]


def project_body(t0, t1, t2, t3, w_ref, v_ref, u_ref, early, front_o, back_o, opp_o, keep_o, both):
    del early
    _, z = where_am_i()
    mine = w_ref[pl.ds(pl.multiple_of(UNIT * (1 - z), HALF), HALF), :]
    both[pl.ds(pl.multiple_of(HALF * z, HALF), HALF), :] = mine
    both[pl.ds(pl.multiple_of(HALF * (1 - z), HALF), HALF), :] = u_ref[...]
    tokens = jnp.concatenate(
        [jnp.concatenate([b[g] for g in range(4)], axis=1) for b in (t0, t1, t2, t3)], axis=0
    )

    def product(weight):
        got = lax.dot_general(tokens, weight, NT, preferred_element_type=F32).astype(BF)
        return [got[ROWS * j : ROWS * (j + 1)] for j in range(4)]

    front = product(w_ref[pl.ds(pl.multiple_of(HALF * z, HALF), UNIT), :])
    mid = product(both[...])
    back = product(v_ref[...])
    for j in range(4):
        front_o[j] = front[j]
        back_o[j] = back[j]
        keep_o[j] = mid[j]
    front_o[4] = mid[1]
    front_o[5] = back[1]
    back_o[4] = mid[3]
    back_o[5] = front[3]
    opp_o[0] = front[2]
    opp_o[1] = mid[2]
    opp_o[2] = back[2]
    keep_o[4] = front[0]
    keep_o[5] = back[0]


def roles(x, z):
    left = 1 + z
    right = 2 - z
    q = jnp.where(x == 0, 0, jnp.where(x == 3, right, left))
    k = jnp.where(x == 0, right, jnp.where(x == 3, left, 0))
    v = jnp.where(x == 0, left, jnp.where(x == 3, 0, right))
    return q, k, v


def attend_body(m_ref, a_ref, b_ref, t0, t1, t2, t3, pn_ref, pf_ref, g_ref, *o_refs):
    x, z = where_am_i()
    gates = g_ref[pl.ds(x ^ 1, 1), :]
    roled = roles(x, z)
    for head in range(3):
        cols = slice(HEAD_DIM * head, HEAD_DIM * (head + 1))

        def part(index, j):
            own = m_ref[j, :, cols]
            behind = a_ref[(j + 1) % 4, :, cols]
            ahead = b_ref[(j + 3) % 4, :, cols]
            return jnp.where(index == 0, own, jnp.where(index == 1, behind, ahead))

        kept = [
            [t[4 + kv, :, cols] for t in (t0, t1, t2, t3)]
            + [pn_ref[i, kv, :, cols] for i in range(3)]
            + [pf_ref[kv, :, cols]]
            for kv in range(2)
        ]
        for j in range(4):
            q, k, v = (part(index, j) for index in roled)
            keys = list(kept[0])
            values = list(kept[1])
            keys[j] = k
            values[j] = v
            scores = lax.dot_general(
                q, jnp.concatenate(keys, axis=0), NT, preferred_element_type=F32
            ) * SCALE
            top = jnp.max(scores, axis=-1, keepdims=True)
            weights = jnp.exp(scores - top)
            total = jnp.sum(weights, axis=-1, keepdims=True)
            summed = jnp.dot(
                weights.astype(BF), jnp.concatenate(values, axis=0), preferred_element_type=F32
            )
            o_refs[j][:, cols] = (gates[:, cols] * (summed / total)).astype(BF)


def fresh_body(k_ref, a_ref, b_ref, p_ref, f_ref):
    x, z = where_am_i()
    rows = (
        (0, (k_ref.at[4], k_ref.at[0], k_ref.at[5])),
        (1, (b_ref.at[5], b_ref.at[4], b_ref.at[3])),
        (2, (p_ref.at[0], p_ref.at[1], p_ref.at[2])),
        (3, (a_ref.at[1], a_ref.at[4], a_ref.at[5])),
    )
    for j, refs in rows:
        source = (x + (1 - 2 * z) * j + 4) % 4
        for unit, ref in zip((2 * z, 1, 2 - 2 * z), refs):
            g = 3 * source + unit

            @pl.when(g >= 4)
            def _():
                cols = pl.ds(pl.multiple_of(UNIT * (g % 4), UNIT), UNIT)
                f_ref[0, g // 4 - 1, :, cols] = ref[...]


def finish_body(a0, a1, a2, a3, h_ref, o_ref):
    x, z = where_am_i()
    for j, ref in enumerate((a0, a1, a2, a3)):
        group = ((x + (1 - 2 * z) * j + 4) % 4) ^ 1
        cols = pl.ds(pl.multiple_of(UNIT * group, UNIT), UNIT)
        o_ref[0, :, cols] = (h_ref[0, :, cols].astype(F32) + ref[...].astype(F32)).astype(BF)


def local(hidden, w_qkv, norm_gain, box_vec, gate, box_mask, stale_kv):
    parts = lax.axis_size("dp")
    segments = lax.axis_size("segment")

    def blocks(*lead):
        return jax.ShapeDtypeStruct((*lead, ROWS, UNIT), BF)

    def rows(count):
        return jax.ShapeDtypeStruct((count, D), BF)

    weight = jnp.swapaxes(w_qkv[0], 0, 1)
    t0, b1, b2, b3, lead, rest = call(
        norm_body, (blocks(6), blocks(6), blocks(6), blocks(6), rows(UNIT), rows(HALF)), 6
    )(hidden, norm_gain, box_vec, box_mask, stale_kv, weight)
    lead = lax.ppermute(lead, ("dp", "patch"), far_pairs(parts))
    t3 = lax.ppermute(b1, "patch", x_pairs(1))
    t1 = lax.ppermute(b3, "patch", x_pairs(3))
    t2 = lax.ppermute(b2, "patch", x_pairs(2))
    rest = lax.ppermute(rest, "patch", partner_pairs())
    before = lax.ppermute(hidden, "segment", [(i, (i + 1) % segments) for i in range(segments)])

    near = call(near_body, blocks(3, 2), 3)(t0, t1, t3)
    near = lax.ppermute(near, "patch", partner_pairs())
    far = call(far_body, blocks(2), 1)(t2)
    far = lax.ppermute(far, "patch", partner_pairs())

    front, back, opposite, keep = call(
        project_body,
        (blocks(6), blocks(6), blocks(3), blocks(6)),
        8,
        scratch_shapes=[pltpu.VMEM((UNIT, D), BF)],
    )(t0, t1, t2, t3, weight, lead, rest, before)
    front = lax.ppermute(front, "patch", x_pairs(1))
    back = lax.ppermute(back, "patch", x_pairs(3))
    opposite = lax.ppermute(opposite, "patch", x_pairs(2))

    out = call(attend_body, (blocks(),) * 4, 10)(
        keep, front, back, t0, t1, t2, t3, near, far, gate.reshape(4, UNIT)
    )
    fresh = call(fresh_body, jax.ShapeDtypeStruct((1, 2, ROWS, D), BF), 4)(
        keep, front, back, opposite
    )

    came = []
    for j in range(4):
        pairs = [
            (s * 8 + src, (s + 1) % segments * 8 + dst)
            for s in range(segments)
            for src, dst in x_pairs(j)
        ]
        came.append(lax.ppermute(out[j], ("segment", "patch"), pairs))
    passed = call(finish_body, jax.ShapeDtypeStruct((1, ROWS, D), BF), 5)(
        came[0], came[3], came[2], came[1], before
    )
    return (passed, fresh)


def solution(mesh):
    placed = (
        P(("dp", "segment"), "patch", None),
        P("segment", None, "patch"),
        P("segment", None),
        P("segment", None),
        P(("dp", "segment"), None),
        P(("dp", "segment"), "patch"),
        P(("dp", "segment"), None, "patch", None),
    )
    return jax.shard_map(
        local,
        mesh=mesh,
        in_specs=placed,
        out_specs=(P(("dp", "segment"), "patch", None), P(("dp", "segment"), None, "patch", None)),
        check_vma=False,
    )
```

```python
import jax
import jax.numpy as jnp
from jax import lax
from jax.experimental import pallas as pl
from jax.experimental.pallas import tpu as pltpu
from jax.sharding import PartitionSpec as P

HEAD_DIM = 128
ROWS = 128
D = 1536
UNIT = 384
HALF = 192
SCALE = HEAD_DIM ** (-0.5)
BF = jnp.bfloat16
F32 = jnp.float32
NT = (((1,), (1,)), ((), ()))
VM = pl.BlockSpec(memory_space=pltpu.VMEM)
PARAMS = pltpu.CompilerParams(vmem_limit_bytes=16 * 1024 * 1024)


def spot(x, z):
    return 2 * (x % 4) + z


def ahead(z):
    return 1 - 2 * z


def x_pairs(steps):
    return [(spot(x, z), spot(x + ahead(z) * steps, z)) for x in range(4) for z in range(2)]


def partner_pairs():
    return [(spot(x, z), spot(x, 1 - z)) for x in range(4) for z in range(2)]


def far_pairs(parts):
    pairs = []
    for dp in range(parts):
        for x in range(4):
            for z in range(2):
                there = (2 * dp + z - ahead(z)) % (2 * parts)
                pairs.append((dp * 8 + spot(x, z), (there // 2) * 8 + spot(x, there % 2)))
    return pairs


def where_am_i():
    p = lax.axis_index("patch")
    return p // 2, p % 2


def call(body, out, count, **more):
    return pl.pallas_call(
        body,
        out_shape=out,
        in_specs=[VM] * count,
        out_specs=jax.tree.map(lambda _: VM, out),
        compiler_params=PARAMS,
        **more,
    )


def norm_body(h_hbm, g_hbm, b_hbm, m_hbm, s_hbm, w_hbm, own, b1, b2, lead, rest, *scratch):
    h_ref, g_ref, b_ref, m_ref, s_ref, l_sem, r_sem, *sems = scratch
    x, z = where_am_i()
    copies = [
        pltpu.make_async_copy(src, dst, sem)
        for src, dst, sem in zip(
            (h_hbm, g_hbm, b_hbm, m_hbm, s_hbm), (h_ref, g_ref, b_ref, m_ref, s_ref), sems
        )
    ]
    copies.append(
        pltpu.make_async_copy(
            w_hbm.at[pl.ds(pl.multiple_of(HALF * z, HALF), UNIT), :], lead, l_sem
        )
    )
    copies.append(
        pltpu.make_async_copy(
            w_hbm.at[pl.ds(pl.multiple_of(UNIT * (1 - z), HALF), HALF), :], rest, r_sem
        )
    )
    for copy in copies:
        copy.start()
    for copy in copies[:4]:
        copy.wait()
    h = h_ref[0].astype(F32)
    inverse = lax.rsqrt(jnp.mean(h * h, axis=-1, keepdims=True) + 1e-06)
    mask = jnp.broadcast_to(m_ref[...].astype(F32), (ROWS, ROWS)).T[:, :1]
    normed = (h * inverse * g_ref[...] + mask * b_ref[...]).astype(BF)
    for bundle in (own, b1, b2):
        for g in range(4):
            bundle[g] = normed[:, UNIT * g : UNIT * (g + 1)]
    copies[4].wait()

    def stale(j, kv):
        group = ((x + (1 - 2 * z) * j + 4) % 4) ^ 1
        return s_ref[0, kv, :, pl.ds(pl.multiple_of(UNIT * group, UNIT), UNIT)]

    for kv in range(2):
        own[4 + kv] = stale(0, kv)
        b1[4 + kv] = stale(1, kv)
        b2[4 + kv] = stale(3, kv)
    b1[6] = stale(2, 0)
    b2[6] = stale(2, 1)
    copies[5].wait()
    copies[6].wait()


def pass_body(t1, t3, from1, from3):
    from1[0] = t1[0]
    from1[1] = t1[1]
    from1[2] = t1[6]
    from3[0] = t3[2]
    from3[1] = t3[3]
    from3[2] = t3[6]


def near_body(t0, t1, t3, o_ref):
    for i, ref in enumerate((t0, t1, t3)):
        o_ref[i] = ref[4:6]


def far_body(c_ref, d_ref, after, o_ref):
    del after
    o_ref[0] = d_ref[2]
    o_ref[1] = c_ref[2]


def project_body(t0, t1, c_ref, d_ref, t3, w_ref, v_ref, u_ref, early, *outs):
    del early
    front_o, back_o, opp_o, keep_o, both = outs
    _, z = where_am_i()
    mine = w_ref[pl.ds(pl.multiple_of(UNIT * (1 - z), HALF), HALF), :]
    both[pl.ds(pl.multiple_of(HALF * z, HALF), HALF), :] = mine
    both[pl.ds(pl.multiple_of(HALF * (1 - z), HALF), HALF), :] = u_ref[...]
    placed = [[t[g] for g in range(4)] for t in (t0, t1, t3)]
    placed.insert(2, [c_ref[0], c_ref[1], d_ref[0], d_ref[1]])
    tokens = jnp.concatenate([jnp.concatenate(b, axis=1) for b in placed], axis=0)

    def product(weight):
        got = lax.dot_general(tokens, weight, NT, preferred_element_type=F32).astype(BF)
        return [got[ROWS * j : ROWS * (j + 1)] for j in range(4)]

    front = product(w_ref[pl.ds(pl.multiple_of(HALF * z, HALF), UNIT), :])
    mid = product(both[...])
    back = product(v_ref[...])
    for j in range(4):
        front_o[j] = front[j]
        back_o[j] = back[j]
        keep_o[j] = mid[j]
    front_o[4] = mid[1]
    front_o[5] = back[1]
    back_o[4] = mid[3]
    back_o[5] = front[3]
    opp_o[0] = front[2]
    opp_o[1] = mid[2]
    opp_o[2] = back[2]
    keep_o[4] = front[0]
    keep_o[5] = back[0]


def roles(x, z):
    left = 1 + z
    right = 2 - z
    q = jnp.where(x == 0, 0, jnp.where(x == 3, right, left))
    k = jnp.where(x == 0, right, jnp.where(x == 3, left, 0))
    v = jnp.where(x == 0, left, jnp.where(x == 3, 0, right))
    return q, k, v


def attend_body(m_ref, a_ref, b_ref, t0, t1, c_ref, d_ref, t3, pn_ref, pf_ref, g_ref, *o_refs):
    x, z = where_am_i()
    gates = g_ref[:, pl.ds(pl.multiple_of(UNIT * (x ^ 1), UNIT), UNIT)]
    roled = roles(x, z)
    for head in range(3):
        cols = slice(HEAD_DIM * head, HEAD_DIM * (head + 1))

        def part(index, j):
            own = m_ref[j, :, cols]
            behind = a_ref[(j + 1) % 4, :, cols]
            ahead = b_ref[(j + 3) % 4, :, cols]
            return jnp.where(index == 0, own, jnp.where(index == 1, behind, ahead))

        kept = [
            [t0[4 + kv, :, cols], t1[4 + kv, :, cols]]
            + [(d_ref, c_ref)[kv][2, :, cols], t3[4 + kv, :, cols]]
            + [pn_ref[i, kv, :, cols] for i in range(3)]
            + [pf_ref[kv, :, cols]]
            for kv in range(2)
        ]
        for j in range(4):
            q, k, v = (part(index, j) for index in roled)
            keys = list(kept[0])
            values = list(kept[1])
            keys[j] = k
            values[j] = v
            scores = lax.dot_general(
                q, jnp.concatenate(keys, axis=0), NT, preferred_element_type=F32
            ) * SCALE
            top = jnp.max(scores, axis=-1, keepdims=True)
            weights = jnp.exp(scores - top)
            total = jnp.sum(weights, axis=-1, keepdims=True)
            summed = jnp.dot(
                weights.astype(BF), jnp.concatenate(values, axis=0), preferred_element_type=F32
            )
            o_refs[j][:, cols] = (gates[:, cols] * (summed / total)).astype(BF)


def fresh_body(k_ref, a_ref, b_ref, p_ref, after, f_ref):
    del after
    x, z = where_am_i()
    rows = (
        (0, (k_ref.at[4], k_ref.at[0], k_ref.at[5])),
        (1, (b_ref.at[5], b_ref.at[4], b_ref.at[3])),
        (2, (p_ref.at[0], p_ref.at[1], p_ref.at[2])),
        (3, (a_ref.at[1], a_ref.at[4], a_ref.at[5])),
    )
    for j, refs in rows:
        source = (x + (1 - 2 * z) * j + 4) % 4
        for unit, ref in zip((2 * z, 1, 2 - 2 * z), refs):
            g = 3 * source + unit

            @pl.when(g >= 4)
            def _():
                cols = pl.ds(pl.multiple_of(UNIT * (g % 4), UNIT), UNIT)
                f_ref[0, g // 4 - 1, :, cols] = ref[...]


def finish_body(a0, a1, a2, a3, h_ref, o_ref):
    x, z = where_am_i()
    for j, ref in enumerate((a0, a1, a2, a3)):
        group = ((x + (1 - 2 * z) * j + 4) % 4) ^ 1
        cols = pl.ds(pl.multiple_of(UNIT * group, UNIT), UNIT)
        o_ref[0, :, cols] = (h_ref[0, :, cols].astype(F32) + ref[...].astype(F32)).astype(BF)


def local(hidden, w_qkv, norm_gain, box_vec, gate, box_mask, stale_kv):
    parts = lax.axis_size("dp")
    segments = lax.axis_size("segment")

    def blocks(*lead):
        return jax.ShapeDtypeStruct((*lead, ROWS, UNIT), BF)

    def rows(count):
        return jax.ShapeDtypeStruct((count, D), BF)

    weight = jnp.swapaxes(w_qkv[0], 0, 1)
    t0, t3, t1, lead, rest = pl.pallas_call(
        norm_body,
        out_shape=(blocks(6), blocks(7), blocks(7), rows(UNIT), rows(HALF)),
        in_specs=[pl.BlockSpec(memory_space=pltpu.HBM)] * 6,
        out_specs=(VM,) * 5,
        scratch_shapes=[
            pltpu.VMEM((1, ROWS, D), BF),
            pltpu.VMEM((1, D), F32),
            pltpu.VMEM((1, D), F32),
            pltpu.VMEM((1, ROWS), jnp.int32),
            pltpu.VMEM((1, 2, ROWS, D), BF),
        ]
        + [pltpu.SemaphoreType.DMA] * 7,
        compiler_params=pltpu.CompilerParams(vmem_limit_bytes=60 * 1024 * 1024),
    )(hidden, norm_gain, box_vec, box_mask, stale_kv, weight)
    lead = lax.ppermute(lead, ("dp", "patch"), far_pairs(parts))
    t3 = lax.ppermute(t3, "patch", x_pairs(1))
    t1 = lax.ppermute(t1, "patch", x_pairs(3))
    rest = lax.ppermute(rest, "patch", partner_pairs())
    before = lax.ppermute(hidden, "segment", [(i, (i + 1) % segments) for i in range(segments)])

    t2a, t2b = call(pass_body, (blocks(3), blocks(3)), 2)(t1, t3)
    t2a = lax.ppermute(t2a, "patch", x_pairs(3))
    t2b = lax.ppermute(t2b, "patch", x_pairs(1))
    near = call(near_body, blocks(3, 2), 3)(t0, t1, t3)
    near = lax.ppermute(near, "patch", partner_pairs())
    far = call(far_body, blocks(2), 3)(t2a, t2b, near)
    far = lax.ppermute(far, "patch", partner_pairs())

    front, back, opposite, keep = call(
        project_body,
        (blocks(6), blocks(6), blocks(3), blocks(6)),
        9,
        scratch_shapes=[pltpu.VMEM((UNIT, D), BF)],
    )(t0, t1, t2a, t2b, t3, weight, lead, rest, before)
    front = lax.ppermute(front, "patch", x_pairs(1))
    back = lax.ppermute(back, "patch", x_pairs(3))
    opposite, mark = lax.optimization_barrier((opposite, back[0, :16, :128]))
    opposite = lax.ppermute(opposite, "patch", x_pairs(2))

    out = call(attend_body, (blocks(),) * 4, 11)(
        keep, front, back, t0, t1, t2a, t2b, t3, near, far, gate
    )
    fresh = call(fresh_body, jax.ShapeDtypeStruct((1, 2, ROWS, D), BF), 5)(
        keep, front, back, opposite, mark
    )

    came = []
    for j in range(4):
        pairs = [
            (s * 8 + src, (s + 1) % segments * 8 + dst)
            for s in range(segments)
            for src, dst in x_pairs(j)
        ]
        came.append(lax.ppermute(out[j], ("segment", "patch"), pairs))
    passed = call(finish_body, jax.ShapeDtypeStruct((1, ROWS, D), BF), 5)(
        came[0], came[3], came[2], came[1], before
    )
    return (passed, fresh)


def solution(mesh):
    placed = (
        P(("dp", "segment"), "patch", None),
        P("segment", None, "patch"),
        P("segment", None),
        P("segment", None),
        P(("dp", "segment"), None),
        P(("dp", "segment"), "patch"),
        P(("dp", "segment"), None, "patch", None),
    )
    return jax.shard_map(
        local,
        mesh=mesh,
        in_specs=placed,
        out_specs=(P(("dp", "segment"), "patch", None), P(("dp", "segment"), None, "patch", None)),
        check_vma=False,
    )
```

```python
import jax
import jax.numpy as jnp
from jax import lax
from jax.experimental import pallas as pl
from jax.experimental.pallas import tpu as pltpu
from jax.sharding import PartitionSpec as P

HEAD_DIM = 128
ROWS = 128
D = 1536
UNIT = 384
HALF = 192
SCALE = HEAD_DIM ** (-0.5)
BF = jnp.bfloat16
F32 = jnp.float32
NT = (((1,), (1,)), ((), ()))
VM = pl.BlockSpec(memory_space=pltpu.VMEM)
PARAMS = pltpu.CompilerParams(vmem_limit_bytes=16 * 1024 * 1024)


def spot(x, z):
    return 2 * (x % 4) + z


def ahead(z):
    return 1 - 2 * z


def x_pairs(steps):
    return [(spot(x, z), spot(x + ahead(z) * steps, z)) for x in range(4) for z in range(2)]


def partner_pairs():
    return [(spot(x, z), spot(x, 1 - z)) for x in range(4) for z in range(2)]


def far_pairs(parts):
    pairs = []
    for dp in range(parts):
        for x in range(4):
            for z in range(2):
                there = (2 * dp + z - ahead(z)) % (2 * parts)
                pairs.append((dp * 8 + spot(x, z), (there // 2) * 8 + spot(x, there % 2)))
    return pairs


def where_am_i():
    p = lax.axis_index("patch")
    return p // 2, p % 2


def call(body, out, count, **more):
    return pl.pallas_call(
        body,
        out_shape=out,
        in_specs=[VM] * count,
        out_specs=jax.tree.map(lambda _: VM, out),
        compiler_params=PARAMS,
        **more,
    )


def slot(x, z, j):
    return (x + (1 - 2 * z) * j + 4) % 4


def norm_body(h_hbm, g_hbm, b_hbm, m_hbm, s_hbm, o_ref, *scratch):
    h_ref, g_ref, b_ref, m_ref, s_ref, *sems = scratch
    copies = [
        pltpu.make_async_copy(src, dst, sem)
        for src, dst, sem in zip(
            (h_hbm, g_hbm, b_hbm, m_hbm, s_hbm), (h_ref, g_ref, b_ref, m_ref, s_ref), sems
        )
    ]
    for copy in copies:
        copy.start()
    for copy in copies[:4]:
        copy.wait()
    h = h_ref[0].astype(F32)
    inverse = lax.rsqrt(jnp.mean(h * h, axis=-1, keepdims=True) + 1e-06)
    mask = jnp.broadcast_to(m_ref[...].astype(F32), (ROWS, ROWS)).T[:, :1]
    normed = (h * inverse * g_ref[...] + mask * b_ref[...]).astype(BF)
    for x in range(4):
        for g in range(4):
            o_ref[x, g] = normed[:, UNIT * g : UNIT * (g + 1)]
    copies[4].wait()
    for x in range(4):
        for kv in range(2):
            o_ref[x, 4 + kv] = s_ref[0, kv, :, UNIT * (x ^ 1) : UNIT * ((x ^ 1) + 1)]


def kept_body(t_ref, o_ref):
    for x in range(4):
        o_ref[x] = t_ref[x, 4:6]


def project_body(t_ref, w_ref, n_ref, p_ref, early, front_o, back_o, opp_o, keep_o, other, both):
    del early
    x, z = where_am_i()
    other[: D * 3 // 16] = n_ref[...]
    other[D * 3 // 16 :] = p_ref[...]
    mine = w_ref[pl.ds(pl.multiple_of(UNIT * (1 - z), HALF), HALF), :]
    both[pl.ds(pl.multiple_of(HALF * z, HALF), HALF), :] = mine
    both[pl.ds(pl.multiple_of(HALF * (1 - z), HALF), HALF), :] = other[
        pl.ds(pl.multiple_of(UNIT * z, HALF), HALF), :
    ]
    tokens = jnp.concatenate(
        [
            jnp.concatenate([t_ref[slot(x, z, j), g] for g in range(4)], axis=1)
            for j in range(4)
        ],
        axis=0,
    )

    def product(weight):
        got = lax.dot_general(tokens, weight, NT, preferred_element_type=F32).astype(BF)
        return [got[ROWS * j : ROWS * (j + 1)] for j in range(4)]

    front = product(w_ref[pl.ds(pl.multiple_of(HALF * z, HALF), UNIT), :])
    mid = product(both[...])
    back = product(other[pl.ds(pl.multiple_of(HALF * (1 - z), HALF), UNIT), :])
    for j in range(4):
        front_o[j] = front[j]
        back_o[j] = back[j]
        keep_o[j] = mid[j]
    front_o[4] = mid[1]
    front_o[5] = back[1]
    back_o[4] = mid[3]
    back_o[5] = front[3]
    opp_o[0] = front[2]
    opp_o[1] = mid[2]
    opp_o[2] = back[2]
    keep_o[4] = front[0]
    keep_o[5] = back[0]


def roles(x, z):
    left = 1 + z
    right = 2 - z
    q = jnp.where(x == 0, 0, jnp.where(x == 3, right, left))
    k = jnp.where(x == 0, right, jnp.where(x == 3, left, 0))
    v = jnp.where(x == 0, left, jnp.where(x == 3, 0, right))
    return q, k, v


def attend_body(m_ref, a_ref, b_ref, t_ref, p_ref, g_ref, *o_refs):
    x, z = where_am_i()
    gates = g_ref[:, pl.ds(pl.multiple_of(UNIT * (x ^ 1), UNIT), UNIT)]
    roled = roles(x, z)
    for head in range(3):
        cols = slice(HEAD_DIM * head, HEAD_DIM * (head + 1))

        def part(index, j):
            own = m_ref[j, :, cols]
            behind = a_ref[(j + 1) % 4, :, cols]
            ahead = b_ref[(j + 3) % 4, :, cols]
            return jnp.where(index == 0, own, jnp.where(index == 1, behind, ahead))

        kept = [
            [t_ref[slot(x, z, j), 4 + kv, :, cols] for j in range(4)]
            + [p_ref[j, kv, :, cols] for j in range(4)]
            for kv in range(2)
        ]
        for j in range(4):
            q, k, v = (part(index, j) for index in roled)
            keys = list(kept[0])
            values = list(kept[1])
            keys[j] = k
            values[j] = v
            scores = lax.dot_general(
                q, jnp.concatenate(keys, axis=0), NT, preferred_element_type=F32
            ) * SCALE
            top = jnp.max(scores, axis=-1, keepdims=True)
            weights = jnp.exp(scores - top)
            total = jnp.sum(weights, axis=-1, keepdims=True)
            summed = jnp.dot(
                weights.astype(BF), jnp.concatenate(values, axis=0), preferred_element_type=F32
            )
            o_refs[j][:, cols] = (gates[:, cols] * (summed / total)).astype(BF)


def fresh_body(k_ref, a_ref, b_ref, p_ref, after, f_ref):
    del after
    x, z = where_am_i()
    rows = (
        (0, (k_ref.at[4], k_ref.at[0], k_ref.at[5])),
        (1, (b_ref.at[5], b_ref.at[4], b_ref.at[3])),
        (2, (p_ref.at[0], p_ref.at[1], p_ref.at[2])),
        (3, (a_ref.at[1], a_ref.at[4], a_ref.at[5])),
    )
    for j, refs in rows:
        source = slot(x, z, j)
        for unit, ref in zip((2 * z, 1, 2 - 2 * z), refs):
            g = 3 * source + unit

            @pl.when(g >= 4)
            def _():
                cols = pl.ds(pl.multiple_of(UNIT * (g % 4), UNIT), UNIT)
                f_ref[0, g // 4 - 1, :, cols] = ref[...]


def finish_body(a0, a1, a2, a3, h_ref, o_ref):
    x, z = where_am_i()
    for j, ref in enumerate((a0, a1, a2, a3)):
        group = (slot(x, z, j)) ^ 1
        cols = pl.ds(pl.multiple_of(UNIT * group, UNIT), UNIT)
        o_ref[0, :, cols] = (h_ref[0, :, cols].astype(F32) + ref[...].astype(F32)).astype(BF)


def local(hidden, w_qkv, norm_gain, box_vec, gate, box_mask, stale_kv):
    parts = lax.axis_size("dp")
    segments = lax.axis_size("segment")

    def blocks(*lead):
        return jax.ShapeDtypeStruct((*lead, ROWS, UNIT), BF)

    weight = jnp.swapaxes(w_qkv[0], 0, 1)
    packed = pl.pallas_call(
        norm_body,
        out_shape=blocks(4, 6),
        in_specs=[pl.BlockSpec(memory_space=pltpu.HBM)] * 5,
        out_specs=VM,
        scratch_shapes=[
            pltpu.VMEM((1, ROWS, D), BF),
            pltpu.VMEM((1, D), F32),
            pltpu.VMEM((1, D), F32),
            pltpu.VMEM((1, ROWS), jnp.int32),
            pltpu.VMEM((1, 2, ROWS, D), BF),
        ]
        + [pltpu.SemaphoreType.DMA] * 5,
        compiler_params=pltpu.CompilerParams(vmem_limit_bytes=60 * 1024 * 1024),
    )(hidden, norm_gain, box_vec, box_mask, stale_kv)
    came = lax.all_to_all(
        packed, "patch", 0, 0, axis_index_groups=[[0, 2, 4, 6], [1, 3, 5, 7]]
    )
    half = weight.shape[0] // 2
    first = lax.ppermute(weight[:half], ("dp", "patch"), far_pairs(parts))
    second = lax.ppermute(weight[half:], "patch", partner_pairs())
    before = lax.ppermute(hidden, "segment", [(i, (i + 1) % segments) for i in range(segments)])
    kept = call(kept_body, blocks(4, 2), 1)(came)
    kept = lax.ppermute(kept, "patch", partner_pairs())

    front, back, opposite, keep = call(
        project_body,
        (blocks(6), blocks(6), blocks(3), blocks(6)),
        5,
        scratch_shapes=[pltpu.VMEM((2 * half, D), BF), pltpu.VMEM((UNIT, D), BF)],
    )(came, weight, first, second, before)
    front = lax.ppermute(front, "patch", x_pairs(1))
    back = lax.ppermute(back, "patch", x_pairs(3))
    opposite, mark = lax.optimization_barrier((opposite, back[0, :16, :128]))
    opposite = lax.ppermute(opposite, "patch", x_pairs(2))

    out = call(attend_body, (blocks(),) * 4, 6)(keep, front, back, came, kept, gate)
    fresh = call(fresh_body, jax.ShapeDtypeStruct((1, 2, ROWS, D), BF), 5)(
        keep, front, back, opposite, mark
    )

    came = []
    for j in range(4):
        pairs = [
            (s * 8 + src, (s + 1) % segments * 8 + dst)
            for s in range(segments)
            for src, dst in x_pairs(j)
        ]
        came.append(lax.ppermute(out[j], ("segment", "patch"), pairs))
    passed = call(finish_body, jax.ShapeDtypeStruct((1, ROWS, D), BF), 5)(
        came[0], came[3], came[2], came[1], before
    )
    return (passed, fresh)


def solution(mesh):
    placed = (
        P(("dp", "segment"), "patch", None),
        P("segment", None, "patch"),
        P("segment", None),
        P("segment", None),
        P(("dp", "segment"), None),
        P(("dp", "segment"), "patch"),
        P(("dp", "segment"), None, "patch", None),
    )
    return jax.shard_map(
        local,
        mesh=mesh,
        in_specs=placed,
        out_specs=(P(("dp", "segment"), "patch", None), P(("dp", "segment"), None, "patch", None)),
        check_vma=False,
    )
```

```python
import jax
import jax.numpy as jnp
from jax import lax
from jax.experimental import pallas as pl
from jax.experimental.pallas import tpu as pltpu
from jax.sharding import PartitionSpec as P

HEAD_DIM = 128
ROWS = 128
D = 1536
UNIT = 384
HALF = 192
SCALE = HEAD_DIM ** (-0.5)
BF = jnp.bfloat16
F32 = jnp.float32
NT = (((1,), (1,)), ((), ()))
VM = pl.BlockSpec(memory_space=pltpu.VMEM)
HBM = pl.BlockSpec(memory_space=pltpu.HBM)
ANY = pl.BlockSpec(memory_space=pl.ANY)
MIB = 1024 * 1024
PROJECT_ROOM = 50
PLANES = [[0, 2, 4, 6], [1, 3, 5, 7]]


def spot(x, z):
    return 2 * (x % 4) + z


def ahead(z):
    return 1 - 2 * z


def x_pairs(steps):
    return [(spot(x, z), spot(x + ahead(z) * steps, z)) for x in range(4) for z in range(2)]


def partner_pairs():
    return [(spot(x, z), spot(x, 1 - z)) for x in range(4) for z in range(2)]


def far_pairs(parts):
    pairs = []
    for dp in range(parts):
        for x in range(4):
            for z in range(2):
                there = (2 * dp + z - ahead(z)) % (2 * parts)
                pairs.append((dp * 8 + spot(x, z), (there // 2) * 8 + spot(x, there % 2)))
    return pairs


def where_am_i():
    p = lax.axis_index("patch")
    return p // 2, p % 2


def call(body, out, count, spec=VM, room=16, **more):
    return pl.pallas_call(
        body,
        out_shape=out,
        in_specs=[spec] * count,
        out_specs=jax.tree.map(lambda _: spec, out),
        compiler_params=pltpu.CompilerParams(vmem_limit_bytes=room * MIB),
        **more,
    )


class Copies:
    def __init__(self, sems):
        self.sems = sems
        self.count = 0

    def start(self, source, target):
        copy = pltpu.make_async_copy(source, target, self.sems.at[self.count])
        self.count += 1
        copy.start()
        return copy


def wait_all(copies):
    for copy in copies:
        copy.wait()


def slot(x, z, j):
    return (x + (1 - 2 * z) * j + 4) % 4


def norm_body(h_hbm, g_hbm, b_hbm, m_hbm, s_hbm, w_hbm, o_hbm, v_hbm, u_hbm, *scratch):
    h_ref, g_ref, b_ref, m_ref, n_ref, sems = scratch
    copies = Copies(sems)
    mine = [
        copies.start(src, dst)
        for src, dst in ((h_hbm, h_ref), (g_hbm, g_ref), (b_hbm, b_ref), (m_hbm, m_ref))
    ]
    rest = [
        copies.start(
            s_hbm.at[0, kv, :, UNIT * (x ^ 1) : UNIT * ((x ^ 1) + 1)], o_hbm.at[x, 4 + kv]
        )
        for x in range(4)
        for kv in range(2)
    ]
    rest.append(copies.start(w_hbm.at[:HALF], v_hbm))
    rest.append(copies.start(w_hbm.at[HALF:], u_hbm))
    wait_all(mine)
    h = h_ref[0].astype(F32)
    inverse = lax.rsqrt(jnp.mean(h * h, axis=-1, keepdims=True) + 1e-06)
    mask = jnp.broadcast_to(m_ref[...].astype(F32), (ROWS, ROWS)).T[:, :1]
    normed = (h * inverse * g_ref[...] + mask * b_ref[...]).astype(BF)
    for g in range(4):
        n_ref[g] = normed[:, UNIT * g : UNIT * (g + 1)]
    wait_all([copies.start(n_ref, o_hbm.at[x, :4]) for x in range(4)])
    wait_all(rest)


def project_body(t_hbm, w_hbm, v_hbm, u_hbm, early, f_ref, b_ref, o_ref, k_ref, s_out, *scratch):
    del early
    t_ref, w_ref, other, both, sems = scratch
    x, z = where_am_i()
    copies = Copies(sems)
    first = [copies.start(t_hbm.at[:, :4], t_ref), copies.start(w_hbm, w_ref)]
    second = [copies.start(v_hbm, other.at[:HALF]), copies.start(u_hbm, other.at[HALF:])]
    last = [copies.start(t_hbm.at[:, 4:], s_out)]
    wait_all(first)
    tokens = jnp.concatenate(
        [
            jnp.concatenate([t_ref[slot(x, z, j), g] for g in range(4)], axis=1)
            for j in range(4)
        ],
        axis=0,
    )

    def product(weight):
        got = lax.dot_general(tokens, weight, NT, preferred_element_type=F32).astype(BF)
        return [got[ROWS * j : ROWS * (j + 1)] for j in range(4)]

    front = product(w_ref[pl.ds(pl.multiple_of(HALF * z, HALF), UNIT), :])
    for j in range(4):
        f_ref[j] = front[j]
    k_ref[4] = front[0]
    b_ref[5] = front[3]
    o_ref[0] = front[2]
    wait_all(second)
    back = product(other[pl.ds(pl.multiple_of(HALF * (1 - z), HALF), UNIT), :])
    for j in range(4):
        b_ref[j] = back[j]
    k_ref[5] = back[0]
    f_ref[5] = back[1]
    o_ref[2] = back[2]
    both[pl.ds(pl.multiple_of(HALF * z, HALF), HALF), :] = w_ref[
        pl.ds(pl.multiple_of(UNIT * (1 - z), HALF), HALF), :
    ]
    both[pl.ds(pl.multiple_of(HALF * (1 - z), HALF), HALF), :] = other[
        pl.ds(pl.multiple_of(UNIT * z, HALF), HALF), :
    ]
    mid = product(both[...])
    for j in range(4):
        k_ref[j] = mid[j]
    f_ref[4] = mid[1]
    b_ref[4] = mid[3]
    o_ref[1] = mid[2]
    wait_all(last)


def roles(x, z):
    left = 1 + z
    right = 2 - z
    q = jnp.where(x == 0, 0, jnp.where(x == 3, right, left))
    k = jnp.where(x == 0, right, jnp.where(x == 3, left, 0))
    v = jnp.where(x == 0, left, jnp.where(x == 3, 0, right))
    return q, k, v


def attend_body(m_ref, a_ref, b_ref, s_ref, p_ref, g_ref, *o_refs):
    x, z = where_am_i()
    gates = g_ref[:, pl.ds(pl.multiple_of(UNIT * (x ^ 1), UNIT), UNIT)]
    roled = roles(x, z)
    for head in range(3):
        cols = slice(HEAD_DIM * head, HEAD_DIM * (head + 1))

        def part(index, j):
            own = m_ref[j, :, cols]
            behind = a_ref[(j + 1) % 4, :, cols]
            ahead = b_ref[(j + 3) % 4, :, cols]
            return jnp.where(index == 0, own, jnp.where(index == 1, behind, ahead))

        kept = [
            [s_ref[slot(x, z, j), kv, :, cols] for j in range(4)]
            + [p_ref[j, kv, :, cols] for j in range(4)]
            for kv in range(2)
        ]
        for j in range(4):
            q, k, v = (part(index, j) for index in roled)
            keys = list(kept[0])
            values = list(kept[1])
            keys[j] = k
            values[j] = v
            scores = lax.dot_general(
                q, jnp.concatenate(keys, axis=0), NT, preferred_element_type=F32
            ) * SCALE
            top = jnp.max(scores, axis=-1, keepdims=True)
            weights = jnp.exp(scores - top)
            total = jnp.sum(weights, axis=-1, keepdims=True)
            summed = jnp.dot(
                weights.astype(BF), jnp.concatenate(values, axis=0), preferred_element_type=F32
            )
            o_refs[j][:, cols] = (gates[:, cols] * (summed / total)).astype(BF)


def fresh_body(k_ref, a_ref, b_ref, p_ref, after, f_ref):
    del after
    x, z = where_am_i()
    rows = (
        (0, (k_ref.at[4], k_ref.at[0], k_ref.at[5])),
        (1, (b_ref.at[5], b_ref.at[4], b_ref.at[3])),
        (2, (p_ref.at[0], p_ref.at[1], p_ref.at[2])),
        (3, (a_ref.at[1], a_ref.at[4], a_ref.at[5])),
    )
    for j, refs in rows:
        source = slot(x, z, j)
        for unit, ref in zip((2 * z, 1, 2 - 2 * z), refs):
            g = 3 * source + unit

            @pl.when(g >= 4)
            def _():
                cols = pl.ds(pl.multiple_of(UNIT * (g % 4), UNIT), UNIT)
                f_ref[0, g // 4 - 1, :, cols] = ref[...]


def finish_body(a0, a1, a2, a3, h_ref, o_ref):
    x, z = where_am_i()
    for j, ref in enumerate((a0, a1, a2, a3)):
        group = (slot(x, z, j)) ^ 1
        cols = pl.ds(pl.multiple_of(UNIT * group, UNIT), UNIT)
        o_ref[0, :, cols] = (h_ref[0, :, cols].astype(F32) + ref[...].astype(F32)).astype(BF)


def local(hidden, w_qkv, norm_gain, box_vec, gate, box_mask, stale_kv):
    parts = lax.axis_size("dp")
    segments = lax.axis_size("segment")

    def blocks(*lead):
        return jax.ShapeDtypeStruct((*lead, ROWS, UNIT), BF)

    def rows(count):
        return jax.ShapeDtypeStruct((count, D), BF)

    weight = jnp.swapaxes(w_qkv[0], 0, 1)
    packed, small, large = call(
        norm_body,
        (blocks(4, 6), rows(HALF), rows(UNIT)),
        6,
        HBM,
        60,
        scratch_shapes=[
            pltpu.VMEM((1, ROWS, D), BF),
            pltpu.VMEM((1, D), F32),
            pltpu.VMEM((1, D), F32),
            pltpu.VMEM((1, ROWS), jnp.int32),
            pltpu.VMEM((4, ROWS, UNIT), BF),
            pltpu.SemaphoreType.DMA((18,)),
        ],
    )(hidden, norm_gain, box_vec, box_mask, stale_kv, weight)
    came = lax.all_to_all(packed, "patch", 0, 0, axis_index_groups=PLANES)
    large = lax.ppermute(large, "patch", partner_pairs())
    small = lax.ppermute(small, ("dp", "patch"), far_pairs(parts))
    before = lax.ppermute(hidden, "segment", [(i, (i + 1) % segments) for i in range(segments)])

    front, back, opposite, mid, own = pl.pallas_call(
        project_body,
        out_shape=(blocks(6), blocks(6), blocks(3), blocks(6), blocks(4, 2)),
        in_specs=[ANY] * 5,
        out_specs=(VM, VM, VM, VM, ANY),
        scratch_shapes=[
            pltpu.VMEM((4, 4, ROWS, UNIT), BF),
            pltpu.VMEM((UNIT + HALF, D), BF),
            pltpu.VMEM((UNIT + HALF, D), BF),
            pltpu.VMEM((UNIT, D), BF),
            pltpu.SemaphoreType.DMA((5,)),
        ],
        compiler_params=pltpu.CompilerParams(vmem_limit_bytes=PROJECT_ROOM * MIB),
    )(came, weight, small, large, before)
    other = lax.ppermute(own, "patch", partner_pairs())
    front = lax.ppermute(front, "patch", x_pairs(1))
    back = lax.ppermute(back, "patch", x_pairs(3))
    opposite, mark = lax.optimization_barrier((opposite, back[0, :16, :128]))
    opposite = lax.ppermute(opposite, "patch", x_pairs(2))

    out = call(attend_body, (blocks(),) * 4, 6)(mid, front, back, own, other, gate)
    fresh = call(fresh_body, jax.ShapeDtypeStruct((1, 2, ROWS, D), BF), 5)(
        mid, front, back, opposite, mark
    )

    came = []
    for j in range(4):
        pairs = [
            (s * 8 + src, (s + 1) % segments * 8 + dst)
            for s in range(segments)
            for src, dst in x_pairs(j)
        ]
        came.append(lax.ppermute(out[j], ("segment", "patch"), pairs))
    passed = call(finish_body, jax.ShapeDtypeStruct((1, ROWS, D), BF), 5)(
        came[0], came[3], came[2], came[1], before
    )
    return (passed, fresh)


def solution(mesh):
    placed = (
        P(("dp", "segment"), "patch", None),
        P("segment", None, "patch"),
        P("segment", None),
        P("segment", None),
        P(("dp", "segment"), None),
        P(("dp", "segment"), "patch"),
        P(("dp", "segment"), None, "patch", None),
    )
    return jax.shard_map(
        local,
        mesh=mesh,
        in_specs=placed,
        out_specs=(P(("dp", "segment"), "patch", None), P(("dp", "segment"), None, "patch", None)),
        check_vma=False,
    )
```

```python
import jax
import jax.numpy as jnp
from jax import lax
from jax.experimental import pallas as pl
from jax.experimental.pallas import tpu as pltpu
from jax.sharding import PartitionSpec as P

HEAD_DIM = 128
ROWS = 128
D = 1536
UNIT = 384
HALF = 192
SCALE = HEAD_DIM ** (-0.5)
BF = jnp.bfloat16
F32 = jnp.float32
NT = (((1,), (1,)), ((), ()))
VM = pl.BlockSpec(memory_space=pltpu.VMEM)
HBM = pl.BlockSpec(memory_space=pltpu.HBM)
ANY = pl.BlockSpec(memory_space=pl.ANY)
MIB = 1024 * 1024
PROJECT_ROOM = 50
PLANES = [[0, 2, 4, 6], [1, 3, 5, 7]]


def spot(x, z):
    return 2 * (x % 4) + z


def ahead(z):
    return 1 - 2 * z


def x_pairs(steps):
    return [(spot(x, z), spot(x + ahead(z) * steps, z)) for x in range(4) for z in range(2)]


def partner_pairs():
    return [(spot(x, z), spot(x, 1 - z)) for x in range(4) for z in range(2)]


def far_pairs(parts):
    pairs = []
    for dp in range(parts):
        for x in range(4):
            for z in range(2):
                there = (2 * dp + z - ahead(z)) % (2 * parts)
                pairs.append((dp * 8 + spot(x, z), (there // 2) * 8 + spot(x, there % 2)))
    return pairs


def where_am_i():
    p = lax.axis_index("patch")
    return p // 2, p % 2


def call(body, out, count, spec=VM, room=16, **more):
    return pl.pallas_call(
        body,
        out_shape=out,
        in_specs=[spec] * count,
        out_specs=jax.tree.map(lambda _: spec, out),
        compiler_params=pltpu.CompilerParams(vmem_limit_bytes=room * MIB),
        **more,
    )


class Copies:
    def __init__(self, sems):
        self.sems = sems
        self.count = 0

    def start(self, source, target):
        copy = pltpu.make_async_copy(source, target, self.sems.at[self.count])
        self.count += 1
        copy.start()
        return copy


def wait_all(copies):
    for copy in copies:
        copy.wait()


def slot(x, z, j):
    return (x + (1 - 2 * z) * j + 4) % 4


def norm_body(h_hbm, g_hbm, b_hbm, m_hbm, s_hbm, o_hbm, k0, k1, k2, k3, *scratch):
    h_ref, g_ref, b_ref, m_ref, s_ref, n_ref, sems = scratch
    x, z = where_am_i()
    copies = Copies(sems)
    mine = [
        copies.start(src, dst)
        for src, dst in ((h_hbm, h_ref), (g_hbm, g_ref), (b_hbm, b_ref), (m_hbm, m_ref))
    ]
    stale = copies.start(s_hbm, s_ref)
    wait_all(mine)
    h = h_ref[0].astype(F32)
    inverse = lax.rsqrt(jnp.mean(h * h, axis=-1, keepdims=True) + 1e-06)
    mask = jnp.broadcast_to(m_ref[...].astype(F32), (ROWS, ROWS)).T[:, :1]
    normed = (h * inverse * g_ref[...] + mask * b_ref[...]).astype(BF)
    for g in range(4):
        n_ref[g] = normed[:, UNIT * g : UNIT * (g + 1)]
    out = [copies.start(n_ref, o_hbm.at[i]) for i in range(4)]
    stale.wait()
    for j, target in enumerate((k0, k1, k2, k3)):
        cols = pl.ds(pl.multiple_of(UNIT * (slot(x, z, j) ^ 1), UNIT), UNIT)
        out.append(copies.start(s_ref.at[0, :, :, cols], target))
    wait_all(out)


def pack_body(k0, k1, k2, k3, early, o_ref):
    del early
    for j, ref in enumerate((k0, k1, k2, k3)):
        o_ref[j] = ref[...]


def project_body(t_hbm, w_hbm, v_hbm, u_hbm, early, f_ref, b_ref, o_ref, k_ref, *scratch):
    del early
    t_ref, w_ref, other, both, sems = scratch
    x, z = where_am_i()
    copies = Copies(sems)
    first = [copies.start(t_hbm, t_ref), copies.start(w_hbm, w_ref)]
    second = [copies.start(v_hbm, other.at[:HALF]), copies.start(u_hbm, other.at[HALF:])]
    wait_all(first)
    tokens = jnp.concatenate(
        [
            jnp.concatenate([t_ref[slot(x, z, j), g] for g in range(4)], axis=1)
            for j in range(4)
        ],
        axis=0,
    )

    def product(weight):
        got = lax.dot_general(tokens, weight, NT, preferred_element_type=F32).astype(BF)
        return [got[ROWS * j : ROWS * (j + 1)] for j in range(4)]

    front = product(w_ref[pl.ds(pl.multiple_of(HALF * z, HALF), UNIT), :])
    for j in range(4):
        f_ref[j] = front[j]
    k_ref[4] = front[0]
    b_ref[5] = front[3]
    o_ref[0] = front[2]
    wait_all(second)
    back = product(other[pl.ds(pl.multiple_of(HALF * (1 - z), HALF), UNIT), :])
    for j in range(4):
        b_ref[j] = back[j]
    k_ref[5] = back[0]
    f_ref[5] = back[1]
    o_ref[2] = back[2]
    both[pl.ds(pl.multiple_of(HALF * z, HALF), HALF), :] = w_ref[
        pl.ds(pl.multiple_of(UNIT * (1 - z), HALF), HALF), :
    ]
    both[pl.ds(pl.multiple_of(HALF * (1 - z), HALF), HALF), :] = other[
        pl.ds(pl.multiple_of(UNIT * z, HALF), HALF), :
    ]
    mid = product(both[...])
    for j in range(4):
        k_ref[j] = mid[j]
    f_ref[4] = mid[1]
    b_ref[4] = mid[3]
    o_ref[1] = mid[2]


def roles(x, z):
    left = 1 + z
    right = 2 - z
    q = jnp.where(x == 0, 0, jnp.where(x == 3, right, left))
    k = jnp.where(x == 0, right, jnp.where(x == 3, left, 0))
    v = jnp.where(x == 0, left, jnp.where(x == 3, 0, right))
    return q, k, v


def attend_body(m_ref, a_ref, b_ref, s_ref, p_ref, g_ref, *o_refs):
    x, z = where_am_i()
    gates = g_ref[:, pl.ds(pl.multiple_of(UNIT * (x ^ 1), UNIT), UNIT)]
    roled = roles(x, z)
    for head in range(3):
        cols = slice(HEAD_DIM * head, HEAD_DIM * (head + 1))

        def part(index, j):
            own = m_ref[j, :, cols]
            behind = a_ref[(j + 1) % 4, :, cols]
            ahead = b_ref[(j + 3) % 4, :, cols]
            return jnp.where(index == 0, own, jnp.where(index == 1, behind, ahead))

        kept = [
            [s_ref[j, kv, :, cols] for j in range(4)]
            + [p_ref[j, kv, :, cols] for j in range(4)]
            for kv in range(2)
        ]
        for j in range(4):
            q, k, v = (part(index, j) for index in roled)
            keys = list(kept[0])
            values = list(kept[1])
            keys[j] = k
            values[j] = v
            scores = lax.dot_general(
                q, jnp.concatenate(keys, axis=0), NT, preferred_element_type=F32
            ) * SCALE
            top = jnp.max(scores, axis=-1, keepdims=True)
            weights = jnp.exp(scores - top)
            total = jnp.sum(weights, axis=-1, keepdims=True)
            summed = jnp.dot(
                weights.astype(BF), jnp.concatenate(values, axis=0), preferred_element_type=F32
            )
            o_refs[j][:, cols] = (gates[:, cols] * (summed / total)).astype(BF)


def fresh_body(k_ref, a_ref, b_ref, p_ref, after, f_ref):
    del after
    x, z = where_am_i()
    rows = (
        (0, (k_ref.at[4], k_ref.at[0], k_ref.at[5])),
        (1, (b_ref.at[5], b_ref.at[4], b_ref.at[3])),
        (2, (p_ref.at[0], p_ref.at[1], p_ref.at[2])),
        (3, (a_ref.at[1], a_ref.at[4], a_ref.at[5])),
    )
    for j, refs in rows:
        source = slot(x, z, j)
        for unit, ref in zip((2 * z, 1, 2 - 2 * z), refs):
            g = 3 * source + unit

            @pl.when(g >= 4)
            def _():
                cols = pl.ds(pl.multiple_of(UNIT * (g % 4), UNIT), UNIT)
                f_ref[0, g // 4 - 1, :, cols] = ref[...]


def finish_body(a0, a1, a2, a3, h_ref, o_ref):
    x, z = where_am_i()
    for j, ref in enumerate((a0, a1, a2, a3)):
        group = (slot(x, z, j)) ^ 1
        cols = pl.ds(pl.multiple_of(UNIT * group, UNIT), UNIT)
        o_ref[0, :, cols] = (h_ref[0, :, cols].astype(F32) + ref[...].astype(F32)).astype(BF)


def local(hidden, w_qkv, norm_gain, box_vec, gate, box_mask, stale_kv):
    parts = lax.axis_size("dp")
    segments = lax.axis_size("segment")

    def blocks(*lead):
        return jax.ShapeDtypeStruct((*lead, ROWS, UNIT), BF)

    weight = jnp.swapaxes(w_qkv[0], 0, 1)
    packed, k0, k1, k2, k3 = pl.pallas_call(
        norm_body,
        out_shape=(blocks(4, 4),) + (blocks(2),) * 4,
        in_specs=[HBM] * 5,
        out_specs=(HBM,) * 5,
        scratch_shapes=[
            pltpu.VMEM((1, ROWS, D), BF),
            pltpu.VMEM((1, D), F32),
            pltpu.VMEM((1, D), F32),
            pltpu.VMEM((1, ROWS), jnp.int32),
            pltpu.VMEM((1, 2, ROWS, D), BF),
            pltpu.VMEM((4, ROWS, UNIT), BF),
            pltpu.SemaphoreType.DMA((13,)),
        ],
        compiler_params=pltpu.CompilerParams(vmem_limit_bytes=60 * MIB),
    )(hidden, norm_gain, box_vec, box_mask, stale_kv)
    came = lax.all_to_all(packed, "patch", 0, 0, axis_index_groups=PLANES)
    large = lax.ppermute(weight[HALF:], "patch", partner_pairs())
    small = lax.ppermute(weight[:HALF], ("dp", "patch"), far_pairs(parts))
    k1, k3 = lax.ppermute(k3, "patch", x_pairs(3)), lax.ppermute(k1, "patch", x_pairs(1))
    k2 = lax.ppermute(k2, "patch", x_pairs(2))
    before = lax.ppermute(hidden, "segment", [(i, (i + 1) % segments) for i in range(segments)])
    own = call(pack_body, blocks(4, 2), 5)(k0, k1, k2, k3, before)
    other = lax.ppermute(own, "patch", partner_pairs())

    front, back, opposite, mid = pl.pallas_call(
        project_body,
        out_shape=(blocks(6), blocks(6), blocks(3), blocks(6)),
        in_specs=[ANY] * 5,
        out_specs=(VM,) * 4,
        scratch_shapes=[
            pltpu.VMEM((4, 4, ROWS, UNIT), BF),
            pltpu.VMEM((UNIT + HALF, D), BF),
            pltpu.VMEM((UNIT + HALF, D), BF),
            pltpu.VMEM((UNIT, D), BF),
            pltpu.SemaphoreType.DMA((4,)),
        ],
        compiler_params=pltpu.CompilerParams(vmem_limit_bytes=PROJECT_ROOM * MIB),
    )(came, weight, small, large, own)
    front = lax.ppermute(front, "patch", x_pairs(1))
    back = lax.ppermute(back, "patch", x_pairs(3))
    opposite, mark = lax.optimization_barrier((opposite, back[0, :16, :128]))
    opposite = lax.ppermute(opposite, "patch", x_pairs(2))

    out = call(attend_body, (blocks(),) * 4, 6)(mid, front, back, own, other, gate)
    fresh = call(fresh_body, jax.ShapeDtypeStruct((1, 2, ROWS, D), BF), 5)(
        mid, front, back, opposite, mark
    )

    came = []
    for j in range(4):
        pairs = [
            (s * 8 + src, (s + 1) % segments * 8 + dst)
            for s in range(segments)
            for src, dst in x_pairs(j)
        ]
        came.append(lax.ppermute(out[j], ("segment", "patch"), pairs))
    passed = call(finish_body, jax.ShapeDtypeStruct((1, ROWS, D), BF), 5)(
        came[0], came[3], came[2], came[1], before
    )
    return (passed, fresh)


def solution(mesh):
    placed = (
        P(("dp", "segment"), "patch", None),
        P("segment", None, "patch"),
        P("segment", None),
        P("segment", None),
        P(("dp", "segment"), None),
        P(("dp", "segment"), "patch"),
        P(("dp", "segment"), None, "patch", None),
    )
    return jax.shard_map(
        local,
        mesh=mesh,
        in_specs=placed,
        out_specs=(P(("dp", "segment"), "patch", None), P(("dp", "segment"), None, "patch", None)),
        check_vma=False,
    )
```

```python
import jax
import jax.numpy as jnp
from jax import lax
from jax.experimental import pallas as pl
from jax.experimental.pallas import tpu as pltpu
from jax.sharding import PartitionSpec as P

HEAD_DIM = 128
ROWS = 128
D = 1536
UNIT = 384
HALF = 192
PART = 272
SCALE = HEAD_DIM ** (-0.5)
BF = jnp.bfloat16
F32 = jnp.float32
MARK = jax.ShapeDtypeStruct((8, 128), F32)
NT = (((1,), (1,)), ((), ()))
VM = pl.BlockSpec(memory_space=pltpu.VMEM)
HBM = pl.BlockSpec(memory_space=pltpu.HBM)
PARAMS = pltpu.CompilerParams(vmem_limit_bytes=16 * 1024 * 1024)


def spot(x, z):
    return 2 * (x % 4) + z


def ahead(z):
    return 1 - 2 * z


def x_pairs(steps):
    return [(spot(x, z), spot(x + ahead(z) * steps, z)) for x in range(4) for z in range(2)]


def partner_pairs():
    return [(spot(x, z), spot(x, 1 - z)) for x in range(4) for z in range(2)]


def far_pairs(parts):
    pairs = []
    for dp in range(parts):
        for x in range(4):
            for z in range(2):
                there = (2 * dp + z - ahead(z)) % (2 * parts)
                pairs.append((dp * 8 + spot(x, z), (there // 2) * 8 + spot(x, there % 2)))
    return pairs


def where_am_i():
    p = lax.axis_index("patch")
    return p // 2, p % 2


def call(body, out, count, **more):
    return pl.pallas_call(
        body,
        out_shape=out,
        in_specs=[VM] * count,
        out_specs=jax.tree.map(lambda _: VM, out),
        compiler_params=PARAMS,
        **more,
    )


def norm_body(h_hbm, g_hbm, b_hbm, m_hbm, s_hbm, own, b1, b2, mark, *scratch):
    mark[...] = jnp.zeros_like(mark)
    h_ref, g_ref, b_ref, m_ref, s_ref, *sems = scratch
    x, z = where_am_i()
    copies = [
        pltpu.make_async_copy(src, dst, sem)
        for src, dst, sem in zip(
            (h_hbm, g_hbm, b_hbm, m_hbm, s_hbm), (h_ref, g_ref, b_ref, m_ref, s_ref), sems
        )
    ]
    for copy in copies:
        copy.start()
    for copy in copies[:4]:
        copy.wait()
    h = h_ref[0].astype(F32)
    inverse = lax.rsqrt(jnp.mean(h * h, axis=-1, keepdims=True) + 1e-06)
    mask = jnp.broadcast_to(m_ref[...].astype(F32), (ROWS, ROWS)).T[:, :1]
    normed = (h * inverse * g_ref[...] + mask * b_ref[...]).astype(BF)
    for bundle in (own, b1, b2):
        for g in range(4):
            bundle[g] = normed[:, UNIT * g : UNIT * (g + 1)]
    copies[4].wait()

    def stale(j, kv):
        group = ((x + (1 - 2 * z) * j + 4) % 4) ^ 1
        return s_ref[0, kv, :, pl.ds(pl.multiple_of(UNIT * group, UNIT), UNIT)]

    for kv in range(2):
        own[4 + kv] = stale(0, kv)
        b1[4 + kv] = stale(1, kv)
        b2[4 + kv] = stale(3, kv)
    b1[6] = stale(2, 0)
    b2[6] = stale(2, 1)


def weight_body(w_hbm, after, far_ref, near_ref, sems):
    del after
    copies = [
        pltpu.make_async_copy(w_hbm.at[:PART], far_ref, sems.at[0]),
        pltpu.make_async_copy(w_hbm.at[PART:], near_ref, sems.at[1]),
    ]
    for copy in copies:
        copy.start()
    for copy in copies:
        copy.wait()


def pass_body(t1, t3, from1, from3):
    from1[0] = t1[0]
    from1[1] = t1[1]
    from1[2] = t1[6]
    from3[0] = t3[2]
    from3[1] = t3[3]
    from3[2] = t3[6]


def near_body(t0, t1, t3, o_ref):
    for i, ref in enumerate((t0, t1, t3)):
        o_ref[i] = ref[4:6]


def far_body(c_ref, d_ref, after, o_ref):
    del after
    o_ref[0] = d_ref[2]
    o_ref[1] = c_ref[2]


def project_body(t0, t1, c_ref, d_ref, t3, w_ref, v_ref, u_ref, early, *outs):
    del early
    front_o, back_o, opp_o, keep_o, both, other = outs
    _, z = where_am_i()
    other[:PART] = v_ref[...]
    other[PART:] = u_ref[...]
    mine = w_ref[pl.ds(pl.multiple_of(UNIT * (1 - z), HALF), HALF), :]
    both[pl.ds(pl.multiple_of(HALF * z, HALF), HALF), :] = mine
    both[pl.ds(pl.multiple_of(HALF * (1 - z), HALF), HALF), :] = other[
        pl.ds(pl.multiple_of(UNIT * z, HALF), HALF), :
    ]
    placed = [[t[g] for g in range(4)] for t in (t0, t1, t3)]
    placed.insert(2, [c_ref[0], c_ref[1], d_ref[0], d_ref[1]])
    tokens = jnp.concatenate([jnp.concatenate(b, axis=1) for b in placed], axis=0)

    def product(weight):
        got = lax.dot_general(tokens, weight, NT, preferred_element_type=F32).astype(BF)
        return [got[ROWS * j : ROWS * (j + 1)] for j in range(4)]

    front = product(w_ref[pl.ds(pl.multiple_of(HALF * z, HALF), UNIT), :])
    mid = product(both[...])
    back = product(other[pl.ds(pl.multiple_of(HALF * (1 - z), HALF), UNIT), :])
    for j in range(4):
        front_o[j] = front[j]
        back_o[j] = back[j]
        keep_o[j] = mid[j]
    front_o[4] = mid[1]
    front_o[5] = back[1]
    back_o[4] = mid[3]
    back_o[5] = front[3]
    opp_o[0] = front[2]
    opp_o[1] = mid[2]
    opp_o[2] = back[2]
    keep_o[4] = front[0]
    keep_o[5] = back[0]


def roles(x, z):
    left = 1 + z
    right = 2 - z
    q = jnp.where(x == 0, 0, jnp.where(x == 3, right, left))
    k = jnp.where(x == 0, right, jnp.where(x == 3, left, 0))
    v = jnp.where(x == 0, left, jnp.where(x == 3, 0, right))
    return q, k, v


def attend_body(m_ref, a_ref, b_ref, t0, t1, c_ref, d_ref, t3, pn_ref, pf_ref, g_ref, *o_refs):
    x, z = where_am_i()
    gates = g_ref[:, pl.ds(pl.multiple_of(UNIT * (x ^ 1), UNIT), UNIT)]
    roled = roles(x, z)
    for head in range(3):
        cols = slice(HEAD_DIM * head, HEAD_DIM * (head + 1))

        def part(index, j):
            own = m_ref[j, :, cols]
            behind = a_ref[(j + 1) % 4, :, cols]
            ahead = b_ref[(j + 3) % 4, :, cols]
            return jnp.where(index == 0, own, jnp.where(index == 1, behind, ahead))

        kept = [
            [t0[4 + kv, :, cols], t1[4 + kv, :, cols]]
            + [(d_ref, c_ref)[kv][2, :, cols], t3[4 + kv, :, cols]]
            + [pn_ref[i, kv, :, cols] for i in range(3)]
            + [pf_ref[kv, :, cols]]
            for kv in range(2)
        ]
        for j in range(4):
            q, k, v = (part(index, j) for index in roled)
            keys = list(kept[0])
            values = list(kept[1])
            keys[j] = k
            values[j] = v
            scores = lax.dot_general(
                q, jnp.concatenate(keys, axis=0), NT, preferred_element_type=F32
            ) * SCALE
            top = jnp.max(scores, axis=-1, keepdims=True)
            weights = jnp.exp(scores - top)
            total = jnp.sum(weights, axis=-1, keepdims=True)
            summed = jnp.dot(
                weights.astype(BF), jnp.concatenate(values, axis=0), preferred_element_type=F32
            )
            o_refs[j][:, cols] = (gates[:, cols] * (summed / total)).astype(BF)


def fresh_body(k_ref, a_ref, b_ref, p_ref, after, f_ref, mark):
    del after
    mark[...] = jnp.zeros_like(mark)
    x, z = where_am_i()
    rows = (
        (0, (k_ref.at[4], k_ref.at[0], k_ref.at[5])),
        (1, (b_ref.at[5], b_ref.at[4], b_ref.at[3])),
        (2, (p_ref.at[0], p_ref.at[1], p_ref.at[2])),
        (3, (a_ref.at[1], a_ref.at[4], a_ref.at[5])),
    )
    for j, refs in rows:
        source = (x + (1 - 2 * z) * j + 4) % 4
        for unit, ref in zip((2 * z, 1, 2 - 2 * z), refs):
            g = 3 * source + unit

            @pl.when(g >= 4)
            def _():
                cols = pl.ds(pl.multiple_of(UNIT * (g % 4), UNIT), UNIT)
                f_ref[0, g // 4 - 1, :, cols] = ref[...]


def finish_body(a0, a1, a2, a3, h_ref, after, o_ref):
    del after
    x, z = where_am_i()
    for j, ref in enumerate((a0, a1, a2, a3)):
        group = ((x + (1 - 2 * z) * j + 4) % 4) ^ 1
        cols = pl.ds(pl.multiple_of(UNIT * group, UNIT), UNIT)
        o_ref[0, :, cols] = (h_ref[0, :, cols].astype(F32) + ref[...].astype(F32)).astype(BF)


def local(hidden, w_qkv, norm_gain, box_vec, gate, box_mask, stale_kv):
    parts = lax.axis_size("dp")
    segments = lax.axis_size("segment")

    def blocks(*lead):
        return jax.ShapeDtypeStruct((*lead, ROWS, UNIT), BF)

    def rows(count):
        return jax.ShapeDtypeStruct((count, D), BF)

    weight = jnp.swapaxes(w_qkv[0], 0, 1)
    t0, t3, t1, begun = pl.pallas_call(
        norm_body,
        out_shape=(blocks(6), blocks(7), blocks(7), MARK),
        in_specs=[HBM] * 5,
        out_specs=(VM,) * 4,
        scratch_shapes=[
            pltpu.VMEM((1, ROWS, D), BF),
            pltpu.VMEM((1, D), F32),
            pltpu.VMEM((1, D), F32),
            pltpu.VMEM((1, ROWS), jnp.int32),
            pltpu.VMEM((1, 2, ROWS, D), BF),
        ]
        + [pltpu.SemaphoreType.DMA] * 5,
        compiler_params=pltpu.CompilerParams(vmem_limit_bytes=60 * 1024 * 1024),
    )(hidden, norm_gain, box_vec, box_mask, stale_kv)
    far_rows, near_rows = pl.pallas_call(
        weight_body,
        out_shape=(rows(PART), rows(UNIT + HALF - PART)),
        in_specs=[HBM, VM],
        out_specs=(VM, VM),
        scratch_shapes=[pltpu.SemaphoreType.DMA((2,))],
        compiler_params=PARAMS,
    )(weight, begun)
    t3 = lax.ppermute(t3, "patch", x_pairs(1))
    t1 = lax.ppermute(t1, "patch", x_pairs(3))
    near_rows = lax.ppermute(near_rows, "patch", partner_pairs())
    far_rows = lax.ppermute(far_rows, ("dp", "patch"), far_pairs(parts))
    before = lax.ppermute(hidden, "segment", [(i, (i + 1) % segments) for i in range(segments)])

    t2a, t2b = call(pass_body, (blocks(3), blocks(3)), 2)(t1, t3)
    t2a = lax.ppermute(t2a, "patch", x_pairs(3))
    t2b = lax.ppermute(t2b, "patch", x_pairs(1))
    near = call(near_body, blocks(3, 2), 3)(t0, t1, t3)
    near = lax.ppermute(near, "patch", partner_pairs())
    far = call(far_body, blocks(2), 3)(t2a, t2b, near)
    far = lax.ppermute(far, "patch", partner_pairs())

    front, back, opposite, keep = call(
        project_body,
        (blocks(6), blocks(6), blocks(3), blocks(6)),
        9,
        scratch_shapes=[pltpu.VMEM((UNIT, D), BF), pltpu.VMEM((UNIT + HALF, D), BF)],
    )(t0, t1, t2a, t2b, t3, weight, far_rows, near_rows, before)
    front = lax.ppermute(front, "patch", x_pairs(1))
    back = lax.ppermute(back, "patch", x_pairs(3))
    opposite, mark = lax.optimization_barrier((opposite, back[0, :16, :128]))
    opposite = lax.ppermute(opposite, "patch", x_pairs(2))

    out = call(attend_body, (blocks(),) * 4, 11)(
        keep, front, back, t0, t1, t2a, t2b, t3, near, far, gate
    )
    fresh, done = call(fresh_body, (jax.ShapeDtypeStruct((1, 2, ROWS, D), BF), MARK), 5)(
        keep, front, back, opposite, mark
    )

    came = []
    for j in range(4):
        pairs = [
            (s * 8 + src, (s + 1) % segments * 8 + dst)
            for s in range(segments)
            for src, dst in x_pairs(j)
        ]
        came.append(lax.ppermute(out[j], ("segment", "patch"), pairs))
    passed = call(finish_body, jax.ShapeDtypeStruct((1, ROWS, D), BF), 6)(
        came[0], came[3], came[2], came[1], before, done
    )
    return (passed, fresh)


def solution(mesh):
    placed = (
        P(("dp", "segment"), "patch", None),
        P("segment", None, "patch"),
        P("segment", None),
        P("segment", None),
        P(("dp", "segment"), None),
        P(("dp", "segment"), "patch"),
        P(("dp", "segment"), None, "patch", None),
    )
    return jax.shard_map(
        local,
        mesh=mesh,
        in_specs=placed,
        out_specs=(P(("dp", "segment"), "patch", None), P(("dp", "segment"), None, "patch", None)),
        check_vma=False,
    )
```

```python
import jax
import jax.numpy as jnp
from jax import lax
from jax.experimental import pallas as pl
from jax.experimental.pallas import tpu as pltpu
from jax.sharding import PartitionSpec as P

HEAD_DIM = 128
ROWS = 128
D = 1536
UNIT = 384
HALF = 192
PART = 256
SCALE = HEAD_DIM ** (-0.5) * 1.4426950408889634
BF = jnp.bfloat16
F32 = jnp.float32
MARK = jax.ShapeDtypeStruct((8, 128), F32)
NT = (((1,), (1,)), ((), ()))
VM = pl.BlockSpec(memory_space=pltpu.VMEM)
HBM = pl.BlockSpec(memory_space=pltpu.HBM)
PARAMS = pltpu.CompilerParams(vmem_limit_bytes=16 * 1024 * 1024)


def spot(x, z):
    return 2 * (x % 4) + z


def ahead(z):
    return 1 - 2 * z


def x_pairs(steps):
    return [(spot(x, z), spot(x + ahead(z) * steps, z)) for x in range(4) for z in range(2)]


def partner_pairs():
    return [(spot(x, z), spot(x, 1 - z)) for x in range(4) for z in range(2)]


def far_pairs(parts):
    pairs = []
    for dp in range(parts):
        for x in range(4):
            for z in range(2):
                there = (2 * dp + z - ahead(z)) % (2 * parts)
                pairs.append((dp * 8 + spot(x, z), (there // 2) * 8 + spot(x, there % 2)))
    return pairs


def where_am_i():
    p = lax.axis_index("patch")
    return p // 2, p % 2


def call(body, out, count, **more):
    return pl.pallas_call(
        body,
        out_shape=out,
        in_specs=[VM] * count,
        out_specs=jax.tree.map(lambda _: VM, out),
        compiler_params=PARAMS,
        **more,
    )


def norm_body(h_hbm, g_hbm, b_hbm, m_hbm, s_hbm, own, b1, b2, mark, *scratch):
    mark[...] = jnp.zeros_like(mark)
    h_ref, g_ref, b_ref, m_ref, s_ref, *sems = scratch
    x, z = where_am_i()
    copies = [
        pltpu.make_async_copy(src, dst, sem)
        for src, dst, sem in zip(
            (h_hbm, g_hbm, b_hbm, m_hbm, s_hbm), (h_ref, g_ref, b_ref, m_ref, s_ref), sems
        )
    ]
    for copy in copies:
        copy.start()
    for copy in copies[:4]:
        copy.wait()
    h = h_ref[0].astype(F32)
    inverse = lax.rsqrt(jnp.mean(h * h, axis=-1, keepdims=True) + 1e-06)
    mask = jnp.broadcast_to(m_ref[...].astype(F32), (ROWS, ROWS)).T[:, :1]
    normed = (h * inverse * g_ref[...] + mask * b_ref[...]).astype(BF)
    for bundle in (own, b1, b2):
        for g in range(4):
            bundle[g] = normed[:, UNIT * g : UNIT * (g + 1)]
    copies[4].wait()

    def stale(j, kv):
        group = ((x + (1 - 2 * z) * j + 4) % 4) ^ 1
        return s_ref[0, kv, :, pl.ds(pl.multiple_of(UNIT * group, UNIT), UNIT)]

    for kv in range(2):
        own[4 + kv] = stale(0, kv)
        b1[4 + kv] = stale(1, kv)
        b2[4 + kv] = stale(3, kv)
    b1[6] = stale(2, 0)
    b2[6] = stale(2, 1)


def weight_body(w_hbm, after, far_ref, near_ref, sems):
    del after
    copies = [
        pltpu.make_async_copy(w_hbm.at[:PART], far_ref, sems.at[0]),
        pltpu.make_async_copy(w_hbm.at[PART:], near_ref, sems.at[1]),
    ]
    for copy in copies:
        copy.start()
    for copy in copies:
        copy.wait()


def pass_body(t1, t3, from1, from3):
    from1[0] = t1[0]
    from1[1] = t1[1]
    from1[2] = t1[6]
    from3[0] = t3[2]
    from3[1] = t3[3]
    from3[2] = t3[6]


def near_body(t0, t1, t3, o_ref):
    for i, ref in enumerate((t0, t1, t3)):
        o_ref[i] = ref[4:6]


def far_body(c_ref, d_ref, after, o_ref):
    del after
    o_ref[0] = d_ref[2]
    o_ref[1] = c_ref[2]


def project_body(t0, t1, c_ref, d_ref, t3, w_ref, v_ref, u_ref, early, *outs):
    del early
    front_o, back_o, opp_o, keep_o, both, other = outs
    _, z = where_am_i()
    other[:PART] = v_ref[...]
    other[PART:] = u_ref[...]
    mine = w_ref[pl.ds(pl.multiple_of(UNIT * (1 - z), HALF), HALF), :]
    both[pl.ds(pl.multiple_of(HALF * z, HALF), HALF), :] = mine
    both[pl.ds(pl.multiple_of(HALF * (1 - z), HALF), HALF), :] = other[
        pl.ds(pl.multiple_of(UNIT * z, HALF), HALF), :
    ]
    placed = [[t[g] for g in range(4)] for t in (t0, t1, t3)]
    placed.insert(2, [c_ref[0], c_ref[1], d_ref[0], d_ref[1]])
    tokens = jnp.concatenate([jnp.concatenate(b, axis=1) for b in placed], axis=0)

    def product(weight):
        got = lax.dot_general(tokens, weight, NT, preferred_element_type=F32).astype(BF)
        return [got[ROWS * j : ROWS * (j + 1)] for j in range(4)]

    front = product(w_ref[pl.ds(pl.multiple_of(HALF * z, HALF), UNIT), :])
    mid = product(both[...])
    back = product(other[pl.ds(pl.multiple_of(HALF * (1 - z), HALF), UNIT), :])
    for j in range(4):
        front_o[j] = front[j]
        back_o[j] = back[j]
        keep_o[j] = mid[j]
    front_o[4] = mid[1]
    front_o[5] = back[1]
    back_o[4] = mid[3]
    back_o[5] = front[3]
    opp_o[0] = front[2]
    opp_o[1] = mid[2]
    opp_o[2] = back[2]
    keep_o[4] = front[0]
    keep_o[5] = back[0]


def roles(x, z):
    left = 1 + z
    right = 2 - z
    q = jnp.where(x == 0, 0, jnp.where(x == 3, right, left))
    k = jnp.where(x == 0, right, jnp.where(x == 3, left, 0))
    v = jnp.where(x == 0, left, jnp.where(x == 3, 0, right))
    return q, k, v


def attend_body(m_ref, a_ref, b_ref, t0, t1, c_ref, d_ref, t3, pn_ref, pf_ref, g_ref, *o_refs):
    x, z = where_am_i()
    gates = g_ref[:, pl.ds(pl.multiple_of(UNIT * (x ^ 1), UNIT), UNIT)]
    roled = roles(x, z)
    for head in range(3):
        cols = slice(HEAD_DIM * head, HEAD_DIM * (head + 1))

        def part(index, j):
            own = m_ref[j, :, cols]
            behind = a_ref[(j + 1) % 4, :, cols]
            ahead = b_ref[(j + 3) % 4, :, cols]
            return jnp.where(index == 0, own, jnp.where(index == 1, behind, ahead))

        kept = [
            [t0[4 + kv, :, cols], t1[4 + kv, :, cols]]
            + [(d_ref, c_ref)[kv][2, :, cols], t3[4 + kv, :, cols]]
            + [pn_ref[i, kv, :, cols] for i in range(3)]
            + [pf_ref[kv, :, cols]]
            for kv in range(2)
        ]
        q, k, v = ([part(index, j) for j in range(4)] for index in roled)
        scores = lax.dot_general(
            jnp.concatenate(q, axis=0),
            jnp.concatenate(kept[0], axis=0),
            NT,
            preferred_element_type=F32,
        )
        for j in range(4):
            mine = lax.dot_general(q[j], k[j], NT, preferred_element_type=F32)
            at = ROWS * j
            block = scores[at : at + ROWS]
            parts = [block[:, :at]] if j else []
            block = jnp.concatenate(parts + [mine, block[:, at + ROWS :]], axis=1) * SCALE
            top = jnp.max(block, axis=-1, keepdims=True)
            weights = jnp.exp2(block - top)
            total = jnp.sum(weights, axis=-1, keepdims=True)
            values = list(kept[1])
            values[j] = v[j]
            summed = jnp.dot(
                weights.astype(BF), jnp.concatenate(values, axis=0), preferred_element_type=F32
            )
            o_refs[j][:, cols] = (gates[:, cols] * (summed / total)).astype(BF)


def fresh_body(k_ref, a_ref, b_ref, p_ref, after, f_ref, mark):
    del after
    mark[...] = jnp.zeros_like(mark)
    x, z = where_am_i()
    rows = (
        (0, (k_ref.at[4], k_ref.at[0], k_ref.at[5])),
        (1, (b_ref.at[5], b_ref.at[4], b_ref.at[3])),
        (2, (p_ref.at[0], p_ref.at[1], p_ref.at[2])),
        (3, (a_ref.at[1], a_ref.at[4], a_ref.at[5])),
    )
    for j, refs in rows:
        source = (x + (1 - 2 * z) * j + 4) % 4
        for unit, ref in zip((2 * z, 1, 2 - 2 * z), refs):
            g = 3 * source + unit

            @pl.when(g >= 4)
            def _():
                cols = pl.ds(pl.multiple_of(UNIT * (g % 4), UNIT), UNIT)
                f_ref[0, g // 4 - 1, :, cols] = ref[...]


def finish_body(a0, a1, a2, a3, h_ref, after, o_ref):
    del after
    x, z = where_am_i()
    for j, ref in enumerate((a0, a1, a2, a3)):
        group = ((x + (1 - 2 * z) * j + 4) % 4) ^ 1
        cols = pl.ds(pl.multiple_of(UNIT * group, UNIT), UNIT)
        o_ref[0, :, cols] = (h_ref[0, :, cols].astype(F32) + ref[...].astype(F32)).astype(BF)


def local(hidden, w_qkv, norm_gain, box_vec, gate, box_mask, stale_kv):
    parts = lax.axis_size("dp")
    segments = lax.axis_size("segment")

    def blocks(*lead):
        return jax.ShapeDtypeStruct((*lead, ROWS, UNIT), BF)

    def rows(count):
        return jax.ShapeDtypeStruct((count, D), BF)

    weight = jnp.swapaxes(w_qkv[0], 0, 1)
    t0, t3, t1, begun = pl.pallas_call(
        norm_body,
        out_shape=(blocks(6), blocks(7), blocks(7), MARK),
        in_specs=[HBM] * 5,
        out_specs=(VM,) * 4,
        scratch_shapes=[
            pltpu.VMEM((1, ROWS, D), BF),
            pltpu.VMEM((1, D), F32),
            pltpu.VMEM((1, D), F32),
            pltpu.VMEM((1, ROWS), jnp.int32),
            pltpu.VMEM((1, 2, ROWS, D), BF),
        ]
        + [pltpu.SemaphoreType.DMA] * 5,
        compiler_params=pltpu.CompilerParams(vmem_limit_bytes=60 * 1024 * 1024),
    )(hidden, norm_gain, box_vec, box_mask, stale_kv)
    far_rows, near_rows = pl.pallas_call(
        weight_body,
        out_shape=(rows(PART), rows(UNIT + HALF - PART)),
        in_specs=[HBM, VM],
        out_specs=(VM, VM),
        scratch_shapes=[pltpu.SemaphoreType.DMA((2,))],
        compiler_params=PARAMS,
    )(weight, begun)
    t3 = lax.ppermute(t3, "patch", x_pairs(1))
    t1 = lax.ppermute(t1, "patch", x_pairs(3))
    near_rows = lax.ppermute(near_rows, "patch", partner_pairs())
    far_rows = lax.ppermute(far_rows, ("dp", "patch"), far_pairs(parts))
    before = lax.ppermute(hidden, "segment", [(i, (i + 1) % segments) for i in range(segments)])

    t2a, t2b = call(pass_body, (blocks(3), blocks(3)), 2)(t1, t3)
    t2a = lax.ppermute(t2a, "patch", x_pairs(3))
    t2b = lax.ppermute(t2b, "patch", x_pairs(1))
    near = call(near_body, blocks(3, 2), 3)(t0, t1, t3)
    near = lax.ppermute(near, "patch", partner_pairs())
    far = call(far_body, blocks(2), 3)(t2a, t2b, near)
    far = lax.ppermute(far, "patch", partner_pairs())

    front, back, opposite, keep = call(
        project_body,
        (blocks(6), blocks(6), blocks(3), blocks(6)),
        9,
        scratch_shapes=[pltpu.VMEM((UNIT, D), BF), pltpu.VMEM((UNIT + HALF, D), BF)],
    )(t0, t1, t2a, t2b, t3, weight, far_rows, near_rows, before)
    front = lax.ppermute(front, "patch", x_pairs(1))
    back = lax.ppermute(back, "patch", x_pairs(3))
    opposite, mark = lax.optimization_barrier((opposite, back[0, :16, :128]))
    opposite = lax.ppermute(opposite, "patch", x_pairs(2))

    out = call(attend_body, (blocks(),) * 4, 11)(
        keep, front, back, t0, t1, t2a, t2b, t3, near, far, gate
    )
    fresh, done = call(fresh_body, (jax.ShapeDtypeStruct((1, 2, ROWS, D), BF), MARK), 5)(
        keep, front, back, opposite, mark
    )

    came = []
    for j in range(4):
        pairs = [
            (s * 8 + src, (s + 1) % segments * 8 + dst)
            for s in range(segments)
            for src, dst in x_pairs(j)
        ]
        came.append(lax.ppermute(out[j], ("segment", "patch"), pairs))
    passed = call(finish_body, jax.ShapeDtypeStruct((1, ROWS, D), BF), 6)(
        came[0], came[3], came[2], came[1], before, done
    )
    return (passed, fresh)


def solution(mesh):
    placed = (
        P(("dp", "segment"), "patch", None),
        P("segment", None, "patch"),
        P("segment", None),
        P("segment", None),
        P(("dp", "segment"), None),
        P(("dp", "segment"), "patch"),
        P(("dp", "segment"), None, "patch", None),
    )
    return jax.shard_map(
        local,
        mesh=mesh,
        in_specs=placed,
        out_specs=(P(("dp", "segment"), "patch", None), P(("dp", "segment"), None, "patch", None)),
        check_vma=False,
    )
```

```python
import jax
import jax.numpy as jnp
from jax import lax
from jax.experimental import pallas as pl
from jax.experimental.pallas import tpu as pltpu
from jax.sharding import PartitionSpec as P

HEAD_DIM = 128
ROWS = 128
D = 1536
UNIT = 384
HALF = 192
PART = 256
SCALE = HEAD_DIM ** (-0.5) * 1.4426950408889634
BF = jnp.bfloat16
F32 = jnp.float32
MARK = jax.ShapeDtypeStruct((8, 128), F32)
NT = (((1,), (1,)), ((), ()))
VM = pl.BlockSpec(memory_space=pltpu.VMEM)
HBM = pl.BlockSpec(memory_space=pltpu.HBM)
PARAMS = pltpu.CompilerParams(vmem_limit_bytes=16 * 1024 * 1024)


def spot(x, z):
    return 2 * (x % 4) + z


def ahead(z):
    return 1 - 2 * z


def x_pairs(steps):
    return [(spot(x, z), spot(x + ahead(z) * steps, z)) for x in range(4) for z in range(2)]


def partner_pairs():
    return [(spot(x, z), spot(x, 1 - z)) for x in range(4) for z in range(2)]


def far_pairs(parts):
    pairs = []
    for dp in range(parts):
        for x in range(4):
            for z in range(2):
                there = (2 * dp + z - ahead(z)) % (2 * parts)
                pairs.append((dp * 8 + spot(x, z), (there // 2) * 8 + spot(x, there % 2)))
    return pairs


def where_am_i():
    p = lax.axis_index("patch")
    return p // 2, p % 2


def call(body, out, count, **more):
    return pl.pallas_call(
        body,
        out_shape=out,
        in_specs=[VM] * count,
        out_specs=jax.tree.map(lambda _: VM, out),
        compiler_params=PARAMS,
        **more,
    )


def norm_body(h_hbm, g_hbm, b_hbm, m_hbm, s_hbm, own, b1, b2, mark, *scratch):
    mark[...] = jnp.zeros_like(mark)
    h_ref, g_ref, b_ref, m_ref, s_ref, *sems = scratch
    x, z = where_am_i()
    copies = [
        pltpu.make_async_copy(src, dst, sem)
        for src, dst, sem in zip(
            (h_hbm, g_hbm, b_hbm, m_hbm, s_hbm), (h_ref, g_ref, b_ref, m_ref, s_ref), sems
        )
    ]
    for copy in copies:
        copy.start()
    for copy in copies[:4]:
        copy.wait()
    h = h_ref[0].astype(F32)
    inverse = lax.rsqrt(jnp.mean(h * h, axis=-1, keepdims=True) + 1e-06)
    mask = jnp.broadcast_to(m_ref[...].astype(F32), (ROWS, ROWS)).T[:, :1]
    normed = (h * inverse * g_ref[...] + mask * b_ref[...]).astype(BF)
    for bundle in (own, b1, b2):
        for g in range(4):
            bundle[g] = normed[:, UNIT * g : UNIT * (g + 1)]
    copies[4].wait()

    def stale(j, kv):
        group = ((x + (1 - 2 * z) * j + 4) % 4) ^ 1
        return s_ref[0, kv, :, pl.ds(pl.multiple_of(UNIT * group, UNIT), UNIT)]

    for kv in range(2):
        own[4 + kv] = stale(0, kv)
        b1[4 + kv] = stale(1, kv)
        b2[4 + kv] = stale(3, kv)
    b1[6] = stale(2, 0)
    b2[6] = stale(2, 1)


def weight_body(w_hbm, after, far_ref, near_ref, sems):
    del after
    copies = [
        pltpu.make_async_copy(w_hbm.at[:PART], far_ref, sems.at[0]),
        pltpu.make_async_copy(w_hbm.at[PART:], near_ref, sems.at[1]),
    ]
    for copy in copies:
        copy.start()
    for copy in copies:
        copy.wait()


def pass_body(t1, t3, from1, from3):
    from1[0] = t1[0]
    from1[1] = t1[1]
    from1[2] = t1[6]
    from3[0] = t3[2]
    from3[1] = t3[3]
    from3[2] = t3[6]


def near_body(t0, t1, t3, o_ref):
    for i, ref in enumerate((t0, t1, t3)):
        o_ref[i] = ref[4:6]


def far_body(c_ref, d_ref, after, o_ref):
    del after
    o_ref[0] = d_ref[2]
    o_ref[1] = c_ref[2]


def project_body(t0, t1, c_ref, d_ref, t3, w_ref, v_ref, u_ref, early, *outs):
    del early
    front_o, back_o, opp_o, keep_o, both, other = outs
    _, z = where_am_i()
    other[:PART] = v_ref[...]
    other[PART:] = u_ref[...]
    mine = w_ref[pl.ds(pl.multiple_of(UNIT * (1 - z), HALF), HALF), :]
    both[pl.ds(pl.multiple_of(HALF * z, HALF), HALF), :] = mine
    both[pl.ds(pl.multiple_of(HALF * (1 - z), HALF), HALF), :] = other[
        pl.ds(pl.multiple_of(UNIT * z, HALF), HALF), :
    ]
    placed = [[t[g] for g in range(4)] for t in (t0, t1, t3)]
    placed.insert(2, [c_ref[0], c_ref[1], d_ref[0], d_ref[1]])
    tokens = jnp.concatenate([jnp.concatenate(b, axis=1) for b in placed], axis=0)

    def product(weight):
        got = lax.dot_general(tokens, weight, NT, preferred_element_type=F32).astype(BF)
        return [got[ROWS * j : ROWS * (j + 1)] for j in range(4)]

    front = product(w_ref[pl.ds(pl.multiple_of(HALF * z, HALF), UNIT), :])
    mid = product(both[...])
    back = product(other[pl.ds(pl.multiple_of(HALF * (1 - z), HALF), UNIT), :])
    for j in range(4):
        front_o[j] = front[j]
        back_o[j] = back[j]
        keep_o[j] = mid[j]
    front_o[4] = mid[1]
    front_o[5] = back[1]
    back_o[4] = mid[3]
    back_o[5] = front[3]
    opp_o[0] = front[2]
    opp_o[1] = mid[2]
    opp_o[2] = back[2]
    keep_o[4] = front[0]
    keep_o[5] = back[0]


def roles(x, z):
    left = 1 + z
    right = 2 - z
    q = jnp.where(x == 0, 0, jnp.where(x == 3, right, left))
    k = jnp.where(x == 0, right, jnp.where(x == 3, left, 0))
    v = jnp.where(x == 0, left, jnp.where(x == 3, 0, right))
    return q, k, v


def attend_body(m_ref, a_ref, b_ref, t0, t1, c_ref, d_ref, t3, pn_ref, pf_ref, g_ref, *o_refs):
    x, z = where_am_i()
    gates = g_ref[:, pl.ds(pl.multiple_of(UNIT * (x ^ 1), UNIT), UNIT)]
    roled = roles(x, z)
    units = [(head, j) for head in range(3) for j in range(4)]

    def part(index, j, cols):
        own = m_ref[j, :, cols]
        behind = a_ref[(j + 1) % 4, :, cols]
        ahead = b_ref[(j + 3) % 4, :, cols]
        return jnp.where(index == 0, own, jnp.where(index == 1, behind, ahead))

    def used(kv, j, cols):
        blocks = [t0[4 + kv, :, cols], t1[4 + kv, :, cols]]
        blocks += [(d_ref, c_ref)[kv][2, :, cols], t3[4 + kv, :, cols]]
        blocks += [pn_ref[i, kv, :, cols] for i in range(3)]
        blocks += [pf_ref[kv, :, cols]]
        blocks[j] = part(roled[1 + kv], j, cols)
        return jnp.concatenate(blocks, axis=0)

    def columns(head):
        return slice(HEAD_DIM * head, HEAD_DIM * (head + 1))

    def score(head, j):
        cols = columns(head)
        return lax.dot_general(
            part(roled[0], j, cols), used(0, j, cols), NT, preferred_element_type=F32
        )

    def finish(head, j, weights, total):
        cols = columns(head)
        summed = jnp.dot(weights, used(1, j, cols), preferred_element_type=F32)
        o_refs[j][:, cols] = (gates[:, cols] * (summed * (1.0 / total))).astype(BF)

    coming = score(*units[0])
    behind = None
    for n, unit in enumerate(units):
        scores = coming * SCALE
        if n + 1 < len(units):
            coming = score(*units[n + 1])
        if behind is not None:
            finish(*behind)
        top = jnp.max(scores, axis=-1, keepdims=True)
        weights = jnp.exp2(scores - top)
        behind = (*unit, weights.astype(BF), jnp.sum(weights, axis=-1, keepdims=True))
    finish(*behind)


def fresh_body(k_ref, a_ref, b_ref, p_ref, after, f_ref, mark):
    del after
    mark[...] = jnp.zeros_like(mark)
    x, z = where_am_i()
    rows = (
        (0, (k_ref.at[4], k_ref.at[0], k_ref.at[5])),
        (1, (b_ref.at[5], b_ref.at[4], b_ref.at[3])),
        (2, (p_ref.at[0], p_ref.at[1], p_ref.at[2])),
        (3, (a_ref.at[1], a_ref.at[4], a_ref.at[5])),
    )
    for j, refs in rows:
        source = (x + (1 - 2 * z) * j + 4) % 4
        for unit, ref in zip((2 * z, 1, 2 - 2 * z), refs):
            g = 3 * source + unit

            @pl.when(g >= 4)
            def _():
                cols = pl.ds(pl.multiple_of(UNIT * (g % 4), UNIT), UNIT)
                f_ref[0, g // 4 - 1, :, cols] = ref[...]


def finish_body(a0, a1, a2, a3, h_ref, after, o_ref):
    del after
    x, z = where_am_i()
    for j, ref in enumerate((a0, a1, a2, a3)):
        group = ((x + (1 - 2 * z) * j + 4) % 4) ^ 1
        cols = pl.ds(pl.multiple_of(UNIT * group, UNIT), UNIT)
        o_ref[0, :, cols] = (h_ref[0, :, cols].astype(F32) + ref[...].astype(F32)).astype(BF)


def local(hidden, w_qkv, norm_gain, box_vec, gate, box_mask, stale_kv):
    parts = lax.axis_size("dp")
    segments = lax.axis_size("segment")

    def blocks(*lead):
        return jax.ShapeDtypeStruct((*lead, ROWS, UNIT), BF)

    def rows(count):
        return jax.ShapeDtypeStruct((count, D), BF)

    weight = jnp.swapaxes(w_qkv[0], 0, 1)
    t0, t3, t1, begun = pl.pallas_call(
        norm_body,
        out_shape=(blocks(6), blocks(7), blocks(7), MARK),
        in_specs=[HBM] * 5,
        out_specs=(VM,) * 4,
        scratch_shapes=[
            pltpu.VMEM((1, ROWS, D), BF),
            pltpu.VMEM((1, D), F32),
            pltpu.VMEM((1, D), F32),
            pltpu.VMEM((1, ROWS), jnp.int32),
            pltpu.VMEM((1, 2, ROWS, D), BF),
        ]
        + [pltpu.SemaphoreType.DMA] * 5,
        compiler_params=pltpu.CompilerParams(vmem_limit_bytes=60 * 1024 * 1024),
    )(hidden, norm_gain, box_vec, box_mask, stale_kv)
    far_rows, near_rows = pl.pallas_call(
        weight_body,
        out_shape=(rows(PART), rows(UNIT + HALF - PART)),
        in_specs=[HBM, VM],
        out_specs=(VM, VM),
        scratch_shapes=[pltpu.SemaphoreType.DMA((2,))],
        compiler_params=PARAMS,
    )(weight, begun)
    t3 = lax.ppermute(t3, "patch", x_pairs(1))
    t1 = lax.ppermute(t1, "patch", x_pairs(3))
    near_rows = lax.ppermute(near_rows, "patch", partner_pairs())
    far_rows = lax.ppermute(far_rows, ("dp", "patch"), far_pairs(parts))
    before = lax.ppermute(hidden, "segment", [(i, (i + 1) % segments) for i in range(segments)])

    t2a, t2b = call(pass_body, (blocks(3), blocks(3)), 2)(t1, t3)
    t2a = lax.ppermute(t2a, "patch", x_pairs(3))
    t2b = lax.ppermute(t2b, "patch", x_pairs(1))
    near = call(near_body, blocks(3, 2), 3)(t0, t1, t3)
    near = lax.ppermute(near, "patch", partner_pairs())
    far = call(far_body, blocks(2), 3)(t2a, t2b, near)
    far = lax.ppermute(far, "patch", partner_pairs())

    front, back, opposite, keep = call(
        project_body,
        (blocks(6), blocks(6), blocks(3), blocks(6)),
        9,
        scratch_shapes=[pltpu.VMEM((UNIT, D), BF), pltpu.VMEM((UNIT + HALF, D), BF)],
    )(t0, t1, t2a, t2b, t3, weight, far_rows, near_rows, before)
    front = lax.ppermute(front, "patch", x_pairs(1))
    back = lax.ppermute(back, "patch", x_pairs(3))
    opposite, mark = lax.optimization_barrier((opposite, back[0, :16, :128]))
    opposite = lax.ppermute(opposite, "patch", x_pairs(2))

    out = call(attend_body, (blocks(),) * 4, 11)(
        keep, front, back, t0, t1, t2a, t2b, t3, near, far, gate
    )
    fresh, done = call(fresh_body, (jax.ShapeDtypeStruct((1, 2, ROWS, D), BF), MARK), 5)(
        keep, front, back, opposite, mark
    )

    came = {}
    for j in (2, 1, 3, 0):
        pairs = [
            (s * 8 + src, (s + 1) % segments * 8 + dst)
            for s in range(segments)
            for src, dst in x_pairs(j)
        ]
        came[j] = lax.ppermute(out[j], ("segment", "patch"), pairs)
    passed = call(finish_body, jax.ShapeDtypeStruct((1, ROWS, D), BF), 6)(
        came[0], came[3], came[2], came[1], before, done
    )
    return (passed, fresh)


def solution(mesh):
    placed = (
        P(("dp", "segment"), "patch", None),
        P("segment", None, "patch"),
        P("segment", None),
        P("segment", None),
        P(("dp", "segment"), None),
        P(("dp", "segment"), "patch"),
        P(("dp", "segment"), None, "patch", None),
    )
    return jax.shard_map(
        local,
        mesh=mesh,
        in_specs=placed,
        out_specs=(P(("dp", "segment"), "patch", None), P(("dp", "segment"), None, "patch", None)),
        check_vma=False,
    )
```

```python
import jax
import jax.numpy as jnp
from jax import lax
from jax.experimental import pallas as pl
from jax.experimental.pallas import tpu as pltpu
from jax.sharding import PartitionSpec as P

HEAD_DIM = 128
ROWS = 128
D = 1536
UNIT = 384
HALF = 192
PART = 256
SCALE = HEAD_DIM ** (-0.5) * 1.4426950408889634
BF = jnp.bfloat16
F32 = jnp.float32
MARK = jax.ShapeDtypeStruct((8, 128), F32)
NT = (((1,), (1,)), ((), ()))
VM = pl.BlockSpec(memory_space=pltpu.VMEM)
HBM = pl.BlockSpec(memory_space=pltpu.HBM)
PARAMS = pltpu.CompilerParams(vmem_limit_bytes=16 * 1024 * 1024)


def spot(x, z):
    return 2 * (x % 4) + z


def ahead(z):
    return 1 - 2 * z


def x_pairs(steps):
    return [(spot(x, z), spot(x + ahead(z) * steps, z)) for x in range(4) for z in range(2)]


def partner_pairs():
    return [(spot(x, z), spot(x, 1 - z)) for x in range(4) for z in range(2)]


def far_pairs(parts):
    pairs = []
    for dp in range(parts):
        for x in range(4):
            for z in range(2):
                there = (2 * dp + z - ahead(z)) % (2 * parts)
                pairs.append((dp * 8 + spot(x, z), (there // 2) * 8 + spot(x, there % 2)))
    return pairs


def where_am_i():
    p = lax.axis_index("patch")
    return p // 2, p % 2


def call(body, out, count, **more):
    return pl.pallas_call(
        body,
        out_shape=out,
        in_specs=[VM] * count,
        out_specs=jax.tree.map(lambda _: VM, out),
        compiler_params=PARAMS,
        **more,
    )


def norm_body(h_hbm, g_hbm, b_hbm, m_hbm, s_hbm, own, b1, b2, mark, *scratch):
    mark[...] = jnp.zeros_like(mark)
    h_ref, g_ref, b_ref, m_ref, s_ref, *sems = scratch
    x, z = where_am_i()
    copies = [
        pltpu.make_async_copy(src, dst, sem)
        for src, dst, sem in zip(
            (h_hbm, g_hbm, b_hbm, m_hbm, s_hbm), (h_ref, g_ref, b_ref, m_ref, s_ref), sems
        )
    ]
    for copy in copies:
        copy.start()
    for copy in copies[:4]:
        copy.wait()
    h = h_ref[0].astype(F32)
    inverse = lax.rsqrt(jnp.mean(h * h, axis=-1, keepdims=True) + 1e-06)
    mask = jnp.broadcast_to(m_ref[...].astype(F32), (ROWS, ROWS)).T[:, :1]
    normed = (h * inverse * g_ref[...] + mask * b_ref[...]).astype(BF)
    for bundle in (own, b1, b2):
        for g in range(4):
            bundle[g] = normed[:, UNIT * g : UNIT * (g + 1)]
    copies[4].wait()

    def stale(j, kv):
        group = ((x + (1 - 2 * z) * j + 4) % 4) ^ 1
        return s_ref[0, kv, :, pl.ds(pl.multiple_of(UNIT * group, UNIT), UNIT)]

    for kv in range(2):
        own[4 + kv] = stale(0, kv)
        b1[4 + kv] = stale(1, kv)
        b2[4 + kv] = stale(3, kv)
    b1[6] = stale(2, 0)
    b2[6] = stale(2, 1)


def weight_body(w_hbm, after, far_ref, near_ref, sems):
    del after
    copies = [
        pltpu.make_async_copy(w_hbm.at[:PART], far_ref, sems.at[0]),
        pltpu.make_async_copy(w_hbm.at[PART:], near_ref, sems.at[1]),
    ]
    for copy in copies:
        copy.start()
    for copy in copies:
        copy.wait()


def pass_back_body(t1, o_ref):
    o_ref[0] = t1[0]
    o_ref[1] = t1[1]
    o_ref[2] = t1[6]


def pass_on_body(t3, o_ref):
    o_ref[0] = t3[2]
    o_ref[1] = t3[3]
    o_ref[2] = t3[6]


def near_body(t0, t1, t3, o_ref):
    for i, ref in enumerate((t0, t1, t3)):
        o_ref[i] = ref[4:6]


def far_body(c_ref, d_ref, after, o_ref):
    del after
    o_ref[0] = d_ref[2]
    o_ref[1] = c_ref[2]


def project_body(t0, t1, c_ref, d_ref, t3, w_ref, v_ref, u_ref, early, *outs):
    del early
    front_o, back_o, opp_o, keep_o, both, other = outs
    _, z = where_am_i()
    other[:PART] = v_ref[...]
    other[PART:] = u_ref[...]
    mine = w_ref[pl.ds(pl.multiple_of(UNIT * (1 - z), HALF), HALF), :]
    both[pl.ds(pl.multiple_of(HALF * z, HALF), HALF), :] = mine
    both[pl.ds(pl.multiple_of(HALF * (1 - z), HALF), HALF), :] = other[
        pl.ds(pl.multiple_of(UNIT * z, HALF), HALF), :
    ]
    placed = [[t[g] for g in range(4)] for t in (t0, t1, t3)]
    placed.insert(2, [c_ref[0], c_ref[1], d_ref[0], d_ref[1]])
    tokens = jnp.concatenate([jnp.concatenate(b, axis=1) for b in placed], axis=0)

    def product(weight):
        got = lax.dot_general(tokens, weight, NT, preferred_element_type=F32).astype(BF)
        return [got[ROWS * j : ROWS * (j + 1)] for j in range(4)]

    front = product(w_ref[pl.ds(pl.multiple_of(HALF * z, HALF), UNIT), :])
    mid = product(both[...])
    back = product(other[pl.ds(pl.multiple_of(HALF * (1 - z), HALF), UNIT), :])
    for j in range(4):
        front_o[j] = front[j]
        back_o[j] = back[j]
        keep_o[j] = mid[j]
    front_o[4] = mid[1]
    front_o[5] = back[1]
    back_o[4] = mid[3]
    back_o[5] = front[3]
    opp_o[0] = front[2]
    opp_o[1] = mid[2]
    opp_o[2] = back[2]
    keep_o[4] = front[0]
    keep_o[5] = back[0]


def roles(x, z):
    left = 1 + z
    right = 2 - z
    q = jnp.where(x == 0, 0, jnp.where(x == 3, right, left))
    k = jnp.where(x == 0, right, jnp.where(x == 3, left, 0))
    v = jnp.where(x == 0, left, jnp.where(x == 3, 0, right))
    return q, k, v


def attend_body(m_ref, a_ref, b_ref, t0, t1, c_ref, d_ref, t3, pn_ref, pf_ref, g_ref, *o_refs):
    x, z = where_am_i()
    gates = g_ref[:, pl.ds(pl.multiple_of(UNIT * (x ^ 1), UNIT), UNIT)]
    roled = roles(x, z)
    units = [(head, j) for head in range(3) for j in range(4)]

    def part(index, j, cols):
        own = m_ref[j, :, cols]
        behind = a_ref[(j + 1) % 4, :, cols]
        ahead = b_ref[(j + 3) % 4, :, cols]
        return jnp.where(index == 0, own, jnp.where(index == 1, behind, ahead))

    def used(kv, j, cols):
        blocks = [t0[4 + kv, :, cols], t1[4 + kv, :, cols]]
        blocks += [(d_ref, c_ref)[kv][2, :, cols], t3[4 + kv, :, cols]]
        blocks += [pn_ref[i, kv, :, cols] for i in range(3)]
        blocks += [pf_ref[kv, :, cols]]
        blocks[j] = part(roled[1 + kv], j, cols)
        return jnp.concatenate(blocks, axis=0)

    def columns(head):
        return slice(HEAD_DIM * head, HEAD_DIM * (head + 1))

    def score(head, j):
        cols = columns(head)
        return lax.dot_general(
            part(roled[0], j, cols), used(0, j, cols), NT, preferred_element_type=F32
        )

    def finish(head, j, weights, total):
        cols = columns(head)
        summed = jnp.dot(weights, used(1, j, cols), preferred_element_type=F32)
        o_refs[j][:, cols] = (gates[:, cols] * (summed * (1.0 / total))).astype(BF)

    coming = score(*units[0])
    behind = None
    for n, unit in enumerate(units):
        scores = coming * SCALE
        if n + 1 < len(units):
            coming = score(*units[n + 1])
        if behind is not None:
            finish(*behind)
        top = jnp.max(scores, axis=-1, keepdims=True)
        weights = jnp.exp2(scores - top)
        behind = (*unit, weights.astype(BF), jnp.sum(weights, axis=-1, keepdims=True))
    finish(*behind)


def fresh_body(k_ref, a_ref, b_ref, p_ref, after, f_ref, mark):
    del after
    mark[...] = jnp.zeros_like(mark)
    x, z = where_am_i()
    rows = (
        (0, (k_ref.at[4], k_ref.at[0], k_ref.at[5])),
        (1, (b_ref.at[5], b_ref.at[4], b_ref.at[3])),
        (2, (p_ref.at[0], p_ref.at[1], p_ref.at[2])),
        (3, (a_ref.at[1], a_ref.at[4], a_ref.at[5])),
    )
    for j, refs in rows:
        source = (x + (1 - 2 * z) * j + 4) % 4
        for unit, ref in zip((2 * z, 1, 2 - 2 * z), refs):
            g = 3 * source + unit

            @pl.when(g >= 4)
            def _():
                cols = pl.ds(pl.multiple_of(UNIT * (g % 4), UNIT), UNIT)
                f_ref[0, g // 4 - 1, :, cols] = ref[...]


def finish_body(a0, a1, a2, a3, h_ref, after, o_ref):
    del after
    x, z = where_am_i()
    for j, ref in enumerate((a0, a1, a2, a3)):
        group = ((x + (1 - 2 * z) * j + 4) % 4) ^ 1
        cols = pl.ds(pl.multiple_of(UNIT * group, UNIT), UNIT)
        o_ref[0, :, cols] = (h_ref[0, :, cols].astype(F32) + ref[...].astype(F32)).astype(BF)


def local(hidden, w_qkv, norm_gain, box_vec, gate, box_mask, stale_kv):
    parts = lax.axis_size("dp")
    segments = lax.axis_size("segment")

    def blocks(*lead):
        return jax.ShapeDtypeStruct((*lead, ROWS, UNIT), BF)

    def rows(count):
        return jax.ShapeDtypeStruct((count, D), BF)

    weight = jnp.swapaxes(w_qkv[0], 0, 1)
    t0, t3, t1, begun = pl.pallas_call(
        norm_body,
        out_shape=(blocks(6), blocks(7), blocks(7), MARK),
        in_specs=[HBM] * 5,
        out_specs=(VM,) * 4,
        scratch_shapes=[
            pltpu.VMEM((1, ROWS, D), BF),
            pltpu.VMEM((1, D), F32),
            pltpu.VMEM((1, D), F32),
            pltpu.VMEM((1, ROWS), jnp.int32),
            pltpu.VMEM((1, 2, ROWS, D), BF),
        ]
        + [pltpu.SemaphoreType.DMA] * 5,
        compiler_params=pltpu.CompilerParams(vmem_limit_bytes=60 * 1024 * 1024),
    )(hidden, norm_gain, box_vec, box_mask, stale_kv)
    far_rows, near_rows = pl.pallas_call(
        weight_body,
        out_shape=(rows(PART), rows(UNIT + HALF - PART)),
        in_specs=[HBM, VM],
        out_specs=(VM, VM),
        scratch_shapes=[pltpu.SemaphoreType.DMA((2,))],
        compiler_params=PARAMS,
    )(weight, begun)
    t3 = lax.ppermute(t3, "patch", x_pairs(1))
    t1 = lax.ppermute(t1, "patch", x_pairs(3))
    near_rows = lax.ppermute(near_rows, "patch", partner_pairs())
    far_rows = lax.ppermute(far_rows, ("dp", "patch"), far_pairs(parts))
    before = lax.ppermute(hidden, "segment", [(i, (i + 1) % segments) for i in range(segments)])

    t2a = lax.ppermute(call(pass_back_body, blocks(3), 1)(t1), "patch", x_pairs(3))
    t2b = lax.ppermute(call(pass_on_body, blocks(3), 1)(t3), "patch", x_pairs(1))
    near = call(near_body, blocks(3, 2), 3)(t0, t1, t3)
    near = lax.ppermute(near, "patch", partner_pairs())
    far = call(far_body, blocks(2), 3)(t2a, t2b, near)
    far = lax.ppermute(far, "patch", partner_pairs())

    front, back, opposite, keep = call(
        project_body,
        (blocks(6), blocks(6), blocks(3), blocks(6)),
        9,
        scratch_shapes=[pltpu.VMEM((UNIT, D), BF), pltpu.VMEM((UNIT + HALF, D), BF)],
    )(t0, t1, t2a, t2b, t3, weight, far_rows, near_rows, before)
    front = lax.ppermute(front, "patch", x_pairs(1))
    back = lax.ppermute(back, "patch", x_pairs(3))
    opposite, mark = lax.optimization_barrier((opposite, back[0, :16, :128]))
    opposite = lax.ppermute(opposite, "patch", x_pairs(2))

    out = call(attend_body, (blocks(),) * 4, 11)(
        keep, front, back, t0, t1, t2a, t2b, t3, near, far, gate
    )
    fresh, done = call(fresh_body, (jax.ShapeDtypeStruct((1, 2, ROWS, D), BF), MARK), 5)(
        keep, front, back, opposite, mark
    )

    came = {}
    for j in (2, 1, 3, 0):
        pairs = [
            (s * 8 + src, (s + 1) % segments * 8 + dst)
            for s in range(segments)
            for src, dst in x_pairs(j)
        ]
        came[j] = lax.ppermute(out[j], ("segment", "patch"), pairs)
    passed = call(finish_body, jax.ShapeDtypeStruct((1, ROWS, D), BF), 6)(
        came[0], came[3], came[2], came[1], before, done
    )
    return (passed, fresh)


def solution(mesh):
    placed = (
        P(("dp", "segment"), "patch", None),
        P("segment", None, "patch"),
        P("segment", None),
        P("segment", None),
        P(("dp", "segment"), None),
        P(("dp", "segment"), "patch"),
        P(("dp", "segment"), None, "patch", None),
    )
    return jax.shard_map(
        local,
        mesh=mesh,
        in_specs=placed,
        out_specs=(P(("dp", "segment"), "patch", None), P(("dp", "segment"), None, "patch", None)),
        check_vma=False,
    )
```

```python
import jax
import jax.numpy as jnp
from jax import lax
from jax.experimental import pallas as pl
from jax.experimental.pallas import tpu as pltpu
from jax.sharding import PartitionSpec as P

HEAD_DIM = 128
ROWS = 128
D = 1536
UNIT = 384
HALF = 192
PART = 288
SCALE = HEAD_DIM ** (-0.5) * 1.4426950408889634
BF = jnp.bfloat16
F32 = jnp.float32
MARK = jax.ShapeDtypeStruct((8, 128), F32)
NT = (((1,), (1,)), ((), ()))
VM = pl.BlockSpec(memory_space=pltpu.VMEM)
HBM = pl.BlockSpec(memory_space=pltpu.HBM)
PARAMS = pltpu.CompilerParams(vmem_limit_bytes=16 * 1024 * 1024)


def spot(x, z):
    return 2 * (x % 4) + z


def ahead(z):
    return 1 - 2 * z


def x_pairs(steps):
    return [(spot(x, z), spot(x + ahead(z) * steps, z)) for x in range(4) for z in range(2)]


def partner_pairs():
    return [(spot(x, z), spot(x, 1 - z)) for x in range(4) for z in range(2)]


def far_pairs(parts):
    pairs = []
    for dp in range(parts):
        for x in range(4):
            for z in range(2):
                there = (2 * dp + z - ahead(z)) % (2 * parts)
                pairs.append((dp * 8 + spot(x, z), (there // 2) * 8 + spot(x, there % 2)))
    return pairs


def where_am_i():
    p = lax.axis_index("patch")
    return p // 2, p % 2


def call(body, out, count, **more):
    return pl.pallas_call(
        body,
        out_shape=out,
        in_specs=[VM] * count,
        out_specs=jax.tree.map(lambda _: VM, out),
        compiler_params=PARAMS,
        **more,
    )


def norm_body(h_hbm, g_hbm, b_hbm, m_hbm, s_hbm, own, b1, b2, mark, *scratch):
    mark[...] = jnp.zeros_like(mark)
    h_ref, g_ref, b_ref, m_ref, s_ref, *sems = scratch
    x, z = where_am_i()
    copies = [
        pltpu.make_async_copy(src, dst, sem)
        for src, dst, sem in zip(
            (h_hbm, g_hbm, b_hbm, m_hbm, s_hbm), (h_ref, g_ref, b_ref, m_ref, s_ref), sems
        )
    ]
    for copy in copies:
        copy.start()
    for copy in copies[:4]:
        copy.wait()
    h = h_ref[0].astype(F32)
    inverse = lax.rsqrt(jnp.mean(h * h, axis=-1, keepdims=True) + 1e-06)
    mask = jnp.broadcast_to(m_ref[...].astype(F32), (ROWS, ROWS)).T[:, :1]
    normed = (h * inverse * g_ref[...] + mask * b_ref[...]).astype(BF)
    for bundle in (own, b1, b2):
        for g in range(4):
            bundle[g] = normed[:, UNIT * g : UNIT * (g + 1)]
    copies[4].wait()

    def stale(j, kv):
        group = ((x + (1 - 2 * z) * j + 4) % 4) ^ 1
        return s_ref[0, kv, :, pl.ds(pl.multiple_of(UNIT * group, UNIT), UNIT)]

    for kv in range(2):
        own[4 + kv] = stale(0, kv)
        b1[4 + kv] = stale(1, kv)
        b2[4 + kv] = stale(3, kv)
    b1[6] = stale(2, 0)
    b2[6] = stale(2, 1)


def weight_body(w_hbm, after, far_ref, near_ref, sems):
    del after
    copies = [
        pltpu.make_async_copy(w_hbm.at[:PART], far_ref, sems.at[0]),
        pltpu.make_async_copy(w_hbm.at[PART:], near_ref, sems.at[1]),
    ]
    for copy in copies:
        copy.start()
    for copy in copies:
        copy.wait()


def pass_back_body(t1, o_ref):
    o_ref[0] = t1[0]
    o_ref[1] = t1[1]
    o_ref[2] = t1[6]


def pass_on_body(t3, o_ref):
    o_ref[0] = t3[2]
    o_ref[1] = t3[3]
    o_ref[2] = t3[6]


def near_body(t0, t1, t3, o_ref):
    for i, ref in enumerate((t0, t1, t3)):
        o_ref[i] = ref[4:6]


def far_body(c_ref, d_ref, after, o_ref):
    del after
    o_ref[0] = d_ref[2]
    o_ref[1] = c_ref[2]


def project_body(t0, t1, c_ref, d_ref, t3, w_ref, v_ref, u_ref, early, *outs):
    del early
    front_o, back_o, opp_o, keep_o, both, other = outs
    _, z = where_am_i()
    other[:PART] = v_ref[...]
    other[PART:] = u_ref[...]
    mine = w_ref[pl.ds(pl.multiple_of(UNIT * (1 - z), HALF), HALF), :]
    both[pl.ds(pl.multiple_of(HALF * z, HALF), HALF), :] = mine
    both[pl.ds(pl.multiple_of(HALF * (1 - z), HALF), HALF), :] = other[
        pl.ds(pl.multiple_of(UNIT * z, HALF), HALF), :
    ]
    placed = [[t[g] for g in range(4)] for t in (t0, t1, t3)]
    placed.insert(2, [c_ref[0], c_ref[1], d_ref[0], d_ref[1]])
    tokens = jnp.concatenate([jnp.concatenate(b, axis=1) for b in placed], axis=0)

    def product(weight):
        got = lax.dot_general(tokens, weight, NT, preferred_element_type=F32).astype(BF)
        return [got[ROWS * j : ROWS * (j + 1)] for j in range(4)]

    front = product(w_ref[pl.ds(pl.multiple_of(HALF * z, HALF), UNIT), :])
    mid = product(both[...])
    back = product(other[pl.ds(pl.multiple_of(HALF * (1 - z), HALF), UNIT), :])
    for j in range(4):
        front_o[j] = front[j]
        back_o[j] = back[j]
        keep_o[j] = mid[j]
    front_o[4] = mid[1]
    front_o[5] = back[1]
    back_o[4] = mid[3]
    back_o[5] = front[3]
    opp_o[0] = front[2]
    opp_o[1] = mid[2]
    opp_o[2] = back[2]
    keep_o[4] = front[0]
    keep_o[5] = back[0]


def roles(x, z):
    left = 1 + z
    right = 2 - z
    q = jnp.where(x == 0, 0, jnp.where(x == 3, right, left))
    k = jnp.where(x == 0, right, jnp.where(x == 3, left, 0))
    v = jnp.where(x == 0, left, jnp.where(x == 3, 0, right))
    return q, k, v


def attend_body(m_ref, a_ref, b_ref, t0, t1, c_ref, d_ref, t3, pn_ref, pf_ref, g_ref, *o_refs):
    x, z = where_am_i()
    gates = g_ref[:, pl.ds(pl.multiple_of(UNIT * (x ^ 1), UNIT), UNIT)]
    roled = roles(x, z)
    units = [(head, j) for head in range(3) for j in range(4)]

    def part(index, j, cols):
        own = m_ref[j, :, cols]
        behind = a_ref[(j + 1) % 4, :, cols]
        ahead = b_ref[(j + 3) % 4, :, cols]
        return jnp.where(index == 0, own, jnp.where(index == 1, behind, ahead))

    def used(kv, j, cols):
        blocks = [t0[4 + kv, :, cols], t1[4 + kv, :, cols]]
        blocks += [(d_ref, c_ref)[kv][2, :, cols], t3[4 + kv, :, cols]]
        blocks += [pn_ref[i, kv, :, cols] for i in range(3)]
        blocks += [pf_ref[kv, :, cols]]
        blocks[j] = part(roled[1 + kv], j, cols)
        return jnp.concatenate(blocks, axis=0)

    def columns(head):
        return slice(HEAD_DIM * head, HEAD_DIM * (head + 1))

    def score(head, j):
        cols = columns(head)
        return lax.dot_general(
            part(roled[0], j, cols), used(0, j, cols), NT, preferred_element_type=F32
        )

    def finish(head, j, weights, total):
        cols = columns(head)
        summed = jnp.dot(weights, used(1, j, cols), preferred_element_type=F32)
        o_refs[j][:, cols] = (gates[:, cols] * (summed * (1.0 / total))).astype(BF)

    coming = score(*units[0])
    behind = None
    for n, unit in enumerate(units):
        scores = coming * SCALE
        if n + 1 < len(units):
            coming = score(*units[n + 1])
        if behind is not None:
            finish(*behind)
        top = jnp.max(scores, axis=-1, keepdims=True)
        weights = jnp.exp2(scores - top)
        behind = (*unit, weights.astype(BF), jnp.sum(weights, axis=-1, keepdims=True))
    finish(*behind)


def fresh_body(k_ref, a_ref, b_ref, p_ref, after, f_ref, mark):
    del after
    mark[...] = jnp.zeros_like(mark)
    x, z = where_am_i()
    rows = (
        (0, (k_ref.at[4], k_ref.at[0], k_ref.at[5])),
        (1, (b_ref.at[5], b_ref.at[4], b_ref.at[3])),
        (2, (p_ref.at[0], p_ref.at[1], p_ref.at[2])),
        (3, (a_ref.at[1], a_ref.at[4], a_ref.at[5])),
    )
    for j, refs in rows:
        source = (x + (1 - 2 * z) * j + 4) % 4
        for unit, ref in zip((2 * z, 1, 2 - 2 * z), refs):
            g = 3 * source + unit

            @pl.when(g >= 4)
            def _():
                cols = pl.ds(pl.multiple_of(UNIT * (g % 4), UNIT), UNIT)
                f_ref[0, g // 4 - 1, :, cols] = ref[...]


def finish_body(a0, a1, a2, a3, h_ref, after, o_ref):
    del after
    x, z = where_am_i()
    for j, ref in enumerate((a0, a1, a2, a3)):
        group = ((x + (1 - 2 * z) * j + 4) % 4) ^ 1
        cols = pl.ds(pl.multiple_of(UNIT * group, UNIT), UNIT)
        o_ref[0, :, cols] = (h_ref[0, :, cols].astype(F32) + ref[...].astype(F32)).astype(BF)


def local(hidden, w_qkv, norm_gain, box_vec, gate, box_mask, stale_kv):
    parts = lax.axis_size("dp")
    segments = lax.axis_size("segment")

    def blocks(*lead):
        return jax.ShapeDtypeStruct((*lead, ROWS, UNIT), BF)

    def rows(count):
        return jax.ShapeDtypeStruct((count, D), BF)

    weight = jnp.swapaxes(w_qkv[0], 0, 1)
    t0, t3, t1, begun = pl.pallas_call(
        norm_body,
        out_shape=(blocks(6), blocks(7), blocks(7), MARK),
        in_specs=[HBM] * 5,
        out_specs=(VM,) * 4,
        scratch_shapes=[
            pltpu.VMEM((1, ROWS, D), BF),
            pltpu.VMEM((1, D), F32),
            pltpu.VMEM((1, D), F32),
            pltpu.VMEM((1, ROWS), jnp.int32),
            pltpu.VMEM((1, 2, ROWS, D), BF),
        ]
        + [pltpu.SemaphoreType.DMA] * 5,
        compiler_params=pltpu.CompilerParams(vmem_limit_bytes=60 * 1024 * 1024),
    )(hidden, norm_gain, box_vec, box_mask, stale_kv)
    far_rows, near_rows = pl.pallas_call(
        weight_body,
        out_shape=(rows(PART), rows(UNIT + HALF - PART)),
        in_specs=[HBM, VM],
        out_specs=(VM, VM),
        scratch_shapes=[pltpu.SemaphoreType.DMA((2,))],
        compiler_params=PARAMS,
    )(weight, begun)
    t3 = lax.ppermute(t3, "patch", x_pairs(1))
    t1 = lax.ppermute(t1, "patch", x_pairs(3))
    near_rows = lax.ppermute(near_rows, "patch", partner_pairs())
    far_rows = lax.ppermute(far_rows, ("dp", "patch"), far_pairs(parts))
    before = lax.ppermute(hidden, "segment", [(i, (i + 1) % segments) for i in range(segments)])

    t2a = lax.ppermute(call(pass_back_body, blocks(3), 1)(t1), "patch", x_pairs(3))
    t2b = lax.ppermute(call(pass_on_body, blocks(3), 1)(t3), "patch", x_pairs(1))
    near = call(near_body, blocks(3, 2), 3)(t0, t1, t3)
    near = lax.ppermute(near, "patch", partner_pairs())
    far = call(far_body, blocks(2), 3)(t2a, t2b, near)
    far = lax.ppermute(far, "patch", partner_pairs())

    front, back, opposite, keep = call(
        project_body,
        (blocks(6), blocks(6), blocks(3), blocks(6)),
        9,
        scratch_shapes=[pltpu.VMEM((UNIT, D), BF), pltpu.VMEM((UNIT + HALF, D), BF)],
    )(t0, t1, t2a, t2b, t3, weight, far_rows, near_rows, before)
    front = lax.ppermute(front, "patch", x_pairs(1))
    back = lax.ppermute(back, "patch", x_pairs(3))
    opposite, mark = lax.optimization_barrier((opposite, back[0, :16, :128]))
    opposite = lax.ppermute(opposite, "patch", x_pairs(2))

    out = call(attend_body, (blocks(),) * 4, 11)(
        keep, front, back, t0, t1, t2a, t2b, t3, near, far, gate
    )
    fresh, done = call(fresh_body, (jax.ShapeDtypeStruct((1, 2, ROWS, D), BF), MARK), 5)(
        keep, front, back, opposite, mark
    )

    came = {}
    for j in (2, 1, 3, 0):
        pairs = [
            (s * 8 + src, (s + 1) % segments * 8 + dst)
            for s in range(segments)
            for src, dst in x_pairs(j)
        ]
        came[j] = lax.ppermute(out[j], ("segment", "patch"), pairs)
    passed = call(finish_body, jax.ShapeDtypeStruct((1, ROWS, D), BF), 6)(
        came[0], came[3], came[2], came[1], before, done
    )
    return (passed, fresh)


def solution(mesh):
    placed = (
        P(("dp", "segment"), "patch", None),
        P("segment", None, "patch"),
        P("segment", None),
        P("segment", None),
        P(("dp", "segment"), None),
        P(("dp", "segment"), "patch"),
        P(("dp", "segment"), None, "patch", None),
    )
    return jax.shard_map(
        local,
        mesh=mesh,
        in_specs=placed,
        out_specs=(P(("dp", "segment"), "patch", None), P(("dp", "segment"), None, "patch", None)),
        check_vma=False,
    )
```

```python
import jax
import jax.numpy as jnp
from jax import lax
from jax.experimental import pallas as pl
from jax.experimental.pallas import tpu as pltpu
from jax.sharding import PartitionSpec as P

HEAD_DIM = 128
ROWS = 128
D = 1536
UNIT = 384
HALF = 192
PART = 256
SCALE = HEAD_DIM ** (-0.5) * 1.4426950408889634
BF = jnp.bfloat16
F32 = jnp.float32
MARK = jax.ShapeDtypeStruct((8, 128), F32)
NT = (((1,), (1,)), ((), ()))
VM = pl.BlockSpec(memory_space=pltpu.VMEM)
HBM = pl.BlockSpec(memory_space=pltpu.HBM)
PARAMS = pltpu.CompilerParams(vmem_limit_bytes=16 * 1024 * 1024)


def spot(x, z):
    return 2 * (x % 4) + z


def ahead(z):
    return 1 - 2 * z


def x_pairs(steps):
    return [(spot(x, z), spot(x + ahead(z) * steps, z)) for x in range(4) for z in range(2)]


def partner_pairs():
    return [(spot(x, z), spot(x, 1 - z)) for x in range(4) for z in range(2)]


def far_pairs(parts):
    pairs = []
    for dp in range(parts):
        for x in range(4):
            for z in range(2):
                there = (2 * dp + z - ahead(z)) % (2 * parts)
                pairs.append((dp * 8 + spot(x, z), (there // 2) * 8 + spot(x, there % 2)))
    return pairs


def where_am_i():
    p = lax.axis_index("patch")
    return p // 2, p % 2


def call(body, out, count, **more):
    return pl.pallas_call(
        body,
        out_shape=out,
        in_specs=[VM] * count,
        out_specs=jax.tree.map(lambda _: VM, out),
        compiler_params=PARAMS,
        **more,
    )


def norm_body(h_hbm, g_hbm, b_hbm, m_hbm, s_hbm, own, b1, b2, mark, *scratch):
    mark[...] = jnp.zeros_like(mark)
    h_ref, g_ref, b_ref, m_ref, s_ref, *sems = scratch
    x, z = where_am_i()
    copies = [
        pltpu.make_async_copy(src, dst, sem)
        for src, dst, sem in zip(
            (h_hbm, g_hbm, b_hbm, m_hbm, s_hbm), (h_ref, g_ref, b_ref, m_ref, s_ref), sems
        )
    ]
    for copy in copies:
        copy.start()
    for copy in copies[:4]:
        copy.wait()
    h = h_ref[0].astype(F32)
    inverse = lax.rsqrt(jnp.mean(h * h, axis=-1, keepdims=True) + 1e-06)
    mask = jnp.broadcast_to(m_ref[...].astype(F32), (ROWS, ROWS)).T[:, :1]
    normed = (h * inverse * g_ref[...] + mask * b_ref[...]).astype(BF)
    for bundle in (own, b1, b2):
        for g in range(4):
            bundle[g] = normed[:, UNIT * g : UNIT * (g + 1)]
    copies[4].wait()

    def stale(j, kv):
        group = ((x + (1 - 2 * z) * j + 4) % 4) ^ 1
        return s_ref[0, kv, :, pl.ds(pl.multiple_of(UNIT * group, UNIT), UNIT)]

    for kv in range(2):
        own[4 + kv] = stale(0, kv)
        b1[4 + kv] = stale(1, kv)
        b2[4 + kv] = stale(3, kv)
    b1[6] = stale(2, 0)
    b2[6] = stale(2, 1)


def weight_body(w_hbm, after, far_ref, near_ref, sems):
    del after
    copies = [
        pltpu.make_async_copy(w_hbm.at[:PART], far_ref, sems.at[0]),
        pltpu.make_async_copy(w_hbm.at[PART:], near_ref, sems.at[1]),
    ]
    for copy in copies:
        copy.start()
    for copy in copies:
        copy.wait()


def pass_back_body(t1, o_ref):
    o_ref[0] = t1[0]
    o_ref[1] = t1[1]
    o_ref[2] = t1[6]


def pass_on_body(t3, o_ref):
    o_ref[0] = t3[2]
    o_ref[1] = t3[3]
    o_ref[2] = t3[6]


def near_body(t0, t1, t3, o_ref):
    for i, ref in enumerate((t0, t1, t3)):
        o_ref[i] = ref[4:6]


def far_body(c_ref, d_ref, after, o_ref):
    del after
    o_ref[0] = d_ref[2]
    o_ref[1] = c_ref[2]


def project_body(t0, t1, c_ref, d_ref, t3, w_ref, v_ref, u_ref, *outs):
    front_o, back_o, opp_o, keep_o, both, other = outs
    _, z = where_am_i()
    other[:PART] = v_ref[...]
    other[PART:] = u_ref[...]
    mine = w_ref[pl.ds(pl.multiple_of(UNIT * (1 - z), HALF), HALF), :]
    both[pl.ds(pl.multiple_of(HALF * z, HALF), HALF), :] = mine
    both[pl.ds(pl.multiple_of(HALF * (1 - z), HALF), HALF), :] = other[
        pl.ds(pl.multiple_of(UNIT * z, HALF), HALF), :
    ]
    placed = [[t[g] for g in range(4)] for t in (t0, t1, t3)]
    placed.insert(2, [c_ref[0], c_ref[1], d_ref[0], d_ref[1]])
    tokens = jnp.concatenate([jnp.concatenate(b, axis=1) for b in placed], axis=0)

    def product(weight):
        got = lax.dot_general(tokens, weight, NT, preferred_element_type=F32).astype(BF)
        return [got[ROWS * j : ROWS * (j + 1)] for j in range(4)]

    front = product(w_ref[pl.ds(pl.multiple_of(HALF * z, HALF), UNIT), :])
    mid = product(both[...])
    back = product(other[pl.ds(pl.multiple_of(HALF * (1 - z), HALF), UNIT), :])
    for j in range(4):
        front_o[j] = front[j]
        back_o[j] = back[j]
        keep_o[j] = mid[j]
    front_o[4] = mid[1]
    front_o[5] = back[1]
    back_o[4] = mid[3]
    back_o[5] = front[3]
    opp_o[0] = front[2]
    opp_o[1] = mid[2]
    opp_o[2] = back[2]
    keep_o[4] = front[0]
    keep_o[5] = back[0]


def roles(x, z):
    left = 1 + z
    right = 2 - z
    q = jnp.where(x == 0, 0, jnp.where(x == 3, right, left))
    k = jnp.where(x == 0, right, jnp.where(x == 3, left, 0))
    v = jnp.where(x == 0, left, jnp.where(x == 3, 0, right))
    return q, k, v


def attend_body(m_ref, a_ref, b_ref, t0, t1, c_ref, d_ref, t3, pn_ref, pf_ref, g_ref, h_ref, *o_refs):
    x, z = where_am_i()
    for g in range(4):
        o_refs[0][1 + g] = h_ref[0, :, UNIT * g : UNIT * (g + 1)]
    o_refs = (o_refs[0].at[0], *o_refs[1:])
    gates = g_ref[:, pl.ds(pl.multiple_of(UNIT * (x ^ 1), UNIT), UNIT)]
    roled = roles(x, z)
    units = [(head, j) for head in range(3) for j in range(4)]

    def part(index, j, cols):
        own = m_ref[j, :, cols]
        behind = a_ref[(j + 1) % 4, :, cols]
        ahead = b_ref[(j + 3) % 4, :, cols]
        return jnp.where(index == 0, own, jnp.where(index == 1, behind, ahead))

    def used(kv, j, cols):
        blocks = [t0[4 + kv, :, cols], t1[4 + kv, :, cols]]
        blocks += [(d_ref, c_ref)[kv][2, :, cols], t3[4 + kv, :, cols]]
        blocks += [pn_ref[i, kv, :, cols] for i in range(3)]
        blocks += [pf_ref[kv, :, cols]]
        blocks[j] = part(roled[1 + kv], j, cols)
        return jnp.concatenate(blocks, axis=0)

    def columns(head):
        return slice(HEAD_DIM * head, HEAD_DIM * (head + 1))

    def score(head, j):
        cols = columns(head)
        return lax.dot_general(
            part(roled[0], j, cols), used(0, j, cols), NT, preferred_element_type=F32
        )

    def finish(head, j, weights, total):
        cols = columns(head)
        summed = jnp.dot(weights, used(1, j, cols), preferred_element_type=F32)
        o_refs[j][:, cols] = (gates[:, cols] * (summed * (1.0 / total))).astype(BF)

    coming = score(*units[0])
    behind = None
    for n, unit in enumerate(units):
        scores = coming * SCALE
        if n + 1 < len(units):
            coming = score(*units[n + 1])
        if behind is not None:
            finish(*behind)
        top = jnp.max(scores, axis=-1, keepdims=True)
        weights = jnp.exp2(scores - top)
        behind = (*unit, weights.astype(BF), jnp.sum(weights, axis=-1, keepdims=True))
    finish(*behind)


def fresh_body(k_ref, a_ref, b_ref, p_ref, after, f_ref, mark):
    del after
    mark[...] = jnp.zeros_like(mark)
    x, z = where_am_i()
    rows = (
        (0, (k_ref.at[4], k_ref.at[0], k_ref.at[5])),
        (1, (b_ref.at[5], b_ref.at[4], b_ref.at[3])),
        (2, (p_ref.at[0], p_ref.at[1], p_ref.at[2])),
        (3, (a_ref.at[1], a_ref.at[4], a_ref.at[5])),
    )
    for j, refs in rows:
        source = (x + (1 - 2 * z) * j + 4) % 4
        for unit, ref in zip((2 * z, 1, 2 - 2 * z), refs):
            g = 3 * source + unit

            @pl.when(g >= 4)
            def _():
                cols = pl.ds(pl.multiple_of(UNIT * (g % 4), UNIT), UNIT)
                f_ref[0, g // 4 - 1, :, cols] = ref[...]


def finish_body(a0, a1, a2, a3, after, o_ref):
    del after
    x, z = where_am_i()
    for j, ref in enumerate((a0.at[0], a1, a2, a3)):
        group = ((x + (1 - 2 * z) * j + 4) % 4) ^ 1
        cols = pl.ds(pl.multiple_of(UNIT * group, UNIT), UNIT)
        o_ref[0, :, cols] = (a0[1 + group].astype(F32) + ref[...].astype(F32)).astype(BF)


def local(hidden, w_qkv, norm_gain, box_vec, gate, box_mask, stale_kv):
    parts = lax.axis_size("dp")
    segments = lax.axis_size("segment")

    def blocks(*lead):
        return jax.ShapeDtypeStruct((*lead, ROWS, UNIT), BF)

    def rows(count):
        return jax.ShapeDtypeStruct((count, D), BF)

    weight = jnp.swapaxes(w_qkv[0], 0, 1)
    t0, t3, t1, begun = pl.pallas_call(
        norm_body,
        out_shape=(blocks(6), blocks(7), blocks(7), MARK),
        in_specs=[HBM] * 5,
        out_specs=(VM,) * 4,
        scratch_shapes=[
            pltpu.VMEM((1, ROWS, D), BF),
            pltpu.VMEM((1, D), F32),
            pltpu.VMEM((1, D), F32),
            pltpu.VMEM((1, ROWS), jnp.int32),
            pltpu.VMEM((1, 2, ROWS, D), BF),
        ]
        + [pltpu.SemaphoreType.DMA] * 5,
        compiler_params=pltpu.CompilerParams(vmem_limit_bytes=60 * 1024 * 1024),
    )(hidden, norm_gain, box_vec, box_mask, stale_kv)
    far_rows, near_rows = pl.pallas_call(
        weight_body,
        out_shape=(rows(PART), rows(UNIT + HALF - PART)),
        in_specs=[HBM, VM],
        out_specs=(VM, VM),
        scratch_shapes=[pltpu.SemaphoreType.DMA((2,))],
        compiler_params=PARAMS,
    )(weight, begun)
    t3 = lax.ppermute(t3, "patch", x_pairs(1))
    t1 = lax.ppermute(t1, "patch", x_pairs(3))
    near_rows = lax.ppermute(near_rows, "patch", partner_pairs())
    far_rows = lax.ppermute(far_rows, ("dp", "patch"), far_pairs(parts))
    t2a = lax.ppermute(call(pass_back_body, blocks(3), 1)(t1), "patch", x_pairs(3))
    t2b = lax.ppermute(call(pass_on_body, blocks(3), 1)(t3), "patch", x_pairs(1))
    near = call(near_body, blocks(3, 2), 3)(t0, t1, t3)
    near = lax.ppermute(near, "patch", partner_pairs())
    far = call(far_body, blocks(2), 3)(t2a, t2b, near)
    far = lax.ppermute(far, "patch", partner_pairs())

    front, back, opposite, keep = call(
        project_body,
        (blocks(6), blocks(6), blocks(3), blocks(6)),
        8,
        scratch_shapes=[pltpu.VMEM((UNIT, D), BF), pltpu.VMEM((UNIT + HALF, D), BF)],
    )(t0, t1, t2a, t2b, t3, weight, far_rows, near_rows)
    front = lax.ppermute(front, "patch", x_pairs(1))
    back = lax.ppermute(back, "patch", x_pairs(3))
    opposite, mark = lax.optimization_barrier((opposite, back[0, :16, :128]))
    opposite = lax.ppermute(opposite, "patch", x_pairs(2))

    out = call(attend_body, (blocks(5),) + (blocks(),) * 3, 12)(
        keep, front, back, t0, t1, t2a, t2b, t3, near, far, gate, hidden
    )
    fresh, done = call(fresh_body, (jax.ShapeDtypeStruct((1, 2, ROWS, D), BF), MARK), 5)(
        keep, front, back, opposite, mark
    )

    came = {}
    for j in (0, 2, 1, 3):
        pairs = [
            (s * 8 + src, (s + 1) % segments * 8 + dst)
            for s in range(segments)
            for src, dst in x_pairs(j)
        ]
        came[j] = lax.ppermute(out[j], ("segment", "patch"), pairs)
    passed = call(finish_body, jax.ShapeDtypeStruct((1, ROWS, D), BF), 5)(
        came[0], came[3], came[2], came[1], done
    )
    return (passed, fresh)


def solution(mesh):
    placed = (
        P(("dp", "segment"), "patch", None),
        P("segment", None, "patch"),
        P("segment", None),
        P("segment", None),
        P(("dp", "segment"), None),
        P(("dp", "segment"), "patch"),
        P(("dp", "segment"), None, "patch", None),
    )
    return jax.shard_map(
        local,
        mesh=mesh,
        in_specs=placed,
        out_specs=(P(("dp", "segment"), "patch", None), P(("dp", "segment"), None, "patch", None)),
        check_vma=False,
    )
```

```python
import jax
import jax.numpy as jnp
from jax import lax
from jax.experimental import pallas as pl
from jax.experimental.pallas import tpu as pltpu
from jax.sharding import PartitionSpec as P

HEAD_DIM = 128
ROWS = 128
D = 1536
UNIT = 384
HALF = 192
PART = 256
SCALE = HEAD_DIM ** (-0.5) * 1.4426950408889634
BF = jnp.bfloat16
F32 = jnp.float32
MARK = jax.ShapeDtypeStruct((8, 128), F32)
NT = (((1,), (1,)), ((), ()))
VM = pl.BlockSpec(memory_space=pltpu.VMEM)
HBM = pl.BlockSpec(memory_space=pltpu.HBM)
PARAMS = pltpu.CompilerParams(vmem_limit_bytes=16 * 1024 * 1024)


def spot(x, z):
    return 2 * (x % 4) + z


def ahead(z):
    return 1 - 2 * z


def x_pairs(steps):
    return [(spot(x, z), spot(x + ahead(z) * steps, z)) for x in range(4) for z in range(2)]


def partner_pairs():
    return [(spot(x, z), spot(x, 1 - z)) for x in range(4) for z in range(2)]


def far_pairs(parts):
    pairs = []
    for dp in range(parts):
        for x in range(4):
            for z in range(2):
                there = (2 * dp + z - ahead(z)) % (2 * parts)
                pairs.append((dp * 8 + spot(x, z), (there // 2) * 8 + spot(x, there % 2)))
    return pairs


def where_am_i():
    p = lax.axis_index("patch")
    return p // 2, p % 2


def call(body, out, count, **more):
    return pl.pallas_call(
        body,
        out_shape=out,
        in_specs=[VM] * count,
        out_specs=jax.tree.map(lambda _: VM, out),
        compiler_params=PARAMS,
        **more,
    )


def norm_body(h_hbm, g_hbm, b_hbm, m_hbm, s_hbm, own, b1, b2, mark, *scratch):
    mark[...] = jnp.zeros_like(mark)
    h_ref, g_ref, b_ref, m_ref, s_ref, *sems = scratch
    x, z = where_am_i()
    copies = [
        pltpu.make_async_copy(src, dst, sem)
        for src, dst, sem in zip(
            (h_hbm, g_hbm, b_hbm, m_hbm, s_hbm), (h_ref, g_ref, b_ref, m_ref, s_ref), sems
        )
    ]
    for copy in copies:
        copy.start()
    for copy in copies[:4]:
        copy.wait()
    h = h_ref[0].astype(F32)
    inverse = lax.rsqrt(jnp.mean(h * h, axis=-1, keepdims=True) + 1e-06)
    mask = jnp.broadcast_to(m_ref[...].astype(F32), (ROWS, ROWS)).T[:, :1]
    normed = (h * inverse * g_ref[...] + mask * b_ref[...]).astype(BF)
    for bundle in (own, b1, b2):
        for g in range(4):
            bundle[g] = normed[:, UNIT * g : UNIT * (g + 1)]
    copies[4].wait()

    def stale(j, kv):
        group = ((x + (1 - 2 * z) * j + 4) % 4) ^ 1
        return s_ref[0, kv, :, pl.ds(pl.multiple_of(UNIT * group, UNIT), UNIT)]

    for kv in range(2):
        own[4 + kv] = stale(0, kv)
        b1[4 + kv] = stale(1, kv)
        b2[4 + kv] = stale(3, kv)
    b1[6] = stale(2, 0)
    b2[6] = stale(2, 1)


def weight_body(w_hbm, after, far_ref, near_ref, sems):
    del after
    copies = [
        pltpu.make_async_copy(w_hbm.at[:PART], far_ref, sems.at[0]),
        pltpu.make_async_copy(w_hbm.at[PART:], near_ref, sems.at[1]),
    ]
    for copy in copies:
        copy.start()
    for copy in copies:
        copy.wait()


def pass_back_body(t1, o_ref):
    o_ref[0] = t1[0]
    o_ref[1] = t1[1]
    o_ref[2] = t1[6]


def pass_on_body(t3, o_ref):
    o_ref[0] = t3[2]
    o_ref[1] = t3[3]
    o_ref[2] = t3[6]


def near_body(t0, t1, t3, o_ref):
    for i, ref in enumerate((t0, t1, t3)):
        o_ref[i] = ref[4:6]


def far_body(c_ref, d_ref, after, o_ref):
    del after
    o_ref[0] = d_ref[2]
    o_ref[1] = c_ref[2]


def project_body(t0, t1, c_ref, d_ref, t3, w_ref, v_ref, u_ref, *outs):
    front_o, back_o, opp_o, keep_o, both, other = outs
    _, z = where_am_i()
    other[:PART] = v_ref[...]
    other[PART:] = u_ref[...]
    mine = w_ref[pl.ds(pl.multiple_of(UNIT * (1 - z), HALF), HALF), :]
    both[pl.ds(pl.multiple_of(HALF * z, HALF), HALF), :] = mine
    both[pl.ds(pl.multiple_of(HALF * (1 - z), HALF), HALF), :] = other[
        pl.ds(pl.multiple_of(UNIT * z, HALF), HALF), :
    ]
    placed = [[t[g] for g in range(4)] for t in (t0, t1, t3)]
    placed.insert(2, [c_ref[0], c_ref[1], d_ref[0], d_ref[1]])
    tokens = jnp.concatenate([jnp.concatenate(b, axis=1) for b in placed], axis=0)

    def product(weight):
        got = lax.dot_general(tokens, weight, NT, preferred_element_type=F32).astype(BF)
        return [got[ROWS * j : ROWS * (j + 1)] for j in range(4)]

    front = product(w_ref[pl.ds(pl.multiple_of(HALF * z, HALF), UNIT), :])
    mid = product(both[...])
    back = product(other[pl.ds(pl.multiple_of(HALF * (1 - z), HALF), UNIT), :])
    for j in range(4):
        front_o[j] = front[j]
        back_o[j] = back[j]
        keep_o[j] = mid[j]
    front_o[4] = mid[1]
    front_o[5] = back[1]
    back_o[4] = mid[3]
    back_o[5] = front[3]
    opp_o[0] = front[2]
    opp_o[1] = mid[2]
    opp_o[2] = back[2]
    keep_o[4] = front[0]
    keep_o[5] = back[0]


def roles(x, z):
    left = 1 + z
    right = 2 - z
    q = jnp.where(x == 0, 0, jnp.where(x == 3, right, left))
    k = jnp.where(x == 0, right, jnp.where(x == 3, left, 0))
    v = jnp.where(x == 0, left, jnp.where(x == 3, 0, right))
    return q, k, v


def attend_body(m_ref, a_ref, b_ref, t0, t1, c_ref, d_ref, t3, pn_ref, pf_ref, g_ref, h_ref, *o_refs):
    x, z = where_am_i()
    for g in range(4):
        o_refs[0][1 + g] = h_ref[0, :, UNIT * g : UNIT * (g + 1)]
    o_refs = (o_refs[0].at[0], *o_refs[1:])
    gates = g_ref[:, pl.ds(pl.multiple_of(UNIT * (x ^ 1), UNIT), UNIT)]
    roled = roles(x, z)
    units = [(head, j) for head in range(3) for j in range(4)]

    def part(index, j, cols):
        own = m_ref[j, :, cols]
        behind = a_ref[(j + 1) % 4, :, cols]
        ahead = b_ref[(j + 3) % 4, :, cols]
        return jnp.where(index == 0, own, jnp.where(index == 1, behind, ahead))

    def used(kv, j, cols):
        blocks = [t0[4 + kv, :, cols], t1[4 + kv, :, cols]]
        blocks += [(d_ref, c_ref)[kv][2, :, cols], t3[4 + kv, :, cols]]
        blocks += [pn_ref[i, kv, :, cols] for i in range(3)]
        blocks += [pf_ref[kv, :, cols]]
        blocks[j] = part(roled[1 + kv], j, cols)
        return jnp.concatenate(blocks, axis=0)

    def columns(head):
        return slice(HEAD_DIM * head, HEAD_DIM * (head + 1))

    def score(head, j):
        cols = columns(head)
        return lax.dot_general(
            part(roled[0], j, cols), used(0, j, cols), NT, preferred_element_type=F32
        )

    def finish(head, j, weights, total):
        cols = columns(head)
        summed = jnp.dot(weights, used(1, j, cols), preferred_element_type=F32)
        o_refs[j][:, cols] = (gates[:, cols] * (summed * (1.0 / total))).astype(BF)

    coming = score(*units[0])
    behind = None
    for n, unit in enumerate(units):
        scores = coming * SCALE
        if n + 1 < len(units):
            coming = score(*units[n + 1])
        if behind is not None:
            finish(*behind)
        top = jnp.max(scores, axis=-1, keepdims=True)
        weights = jnp.exp2(scores - top)
        behind = (*unit, weights.astype(BF), jnp.sum(weights, axis=-1, keepdims=True))
    finish(*behind)


def fresh_body(k_ref, a_ref, b_ref, p_ref, after, f_ref, mark):
    del after
    mark[...] = jnp.zeros_like(mark)
    x, z = where_am_i()
    rows = (
        (0, (k_ref.at[4], k_ref.at[0], k_ref.at[5])),
        (1, (b_ref.at[5], b_ref.at[4], b_ref.at[3])),
        (2, (p_ref.at[0], p_ref.at[1], p_ref.at[2])),
        (3, (a_ref.at[1], a_ref.at[4], a_ref.at[5])),
    )
    for j, refs in rows:
        source = (x + (1 - 2 * z) * j + 4) % 4
        for unit, ref in zip((2 * z, 1, 2 - 2 * z), refs):
            g = 3 * source + unit

            @pl.when(g >= 4)
            def _():
                cols = pl.ds(pl.multiple_of(UNIT * (g % 4), UNIT), UNIT)
                f_ref[0, g // 4 - 1, :, cols] = ref[...]


def finish_body(a0, a1, a2, a3, after, o_ref):
    del after
    x, z = where_am_i()
    for j, ref in enumerate((a0.at[0], a1, a2, a3)):
        group = ((x + (1 - 2 * z) * j + 4) % 4) ^ 1
        cols = pl.ds(pl.multiple_of(UNIT * group, UNIT), UNIT)
        o_ref[0, :, cols] = (a0[1 + group].astype(F32) + ref[...].astype(F32)).astype(BF)


def local(hidden, w_qkv, norm_gain, box_vec, gate, box_mask, stale_kv):
    parts = lax.axis_size("dp")
    segments = lax.axis_size("segment")

    def blocks(*lead):
        return jax.ShapeDtypeStruct((*lead, ROWS, UNIT), BF)

    def rows(count):
        return jax.ShapeDtypeStruct((count, D), BF)

    weight = jnp.swapaxes(w_qkv[0], 0, 1)
    t0, t3, t1, begun = pl.pallas_call(
        norm_body,
        out_shape=(blocks(6), blocks(7), blocks(7), MARK),
        in_specs=[HBM] * 5,
        out_specs=(VM,) * 4,
        scratch_shapes=[
            pltpu.VMEM((1, ROWS, D), BF),
            pltpu.VMEM((1, D), F32),
            pltpu.VMEM((1, D), F32),
            pltpu.VMEM((1, ROWS), jnp.int32),
            pltpu.VMEM((1, 2, ROWS, D), BF),
        ]
        + [pltpu.SemaphoreType.DMA] * 5,
        compiler_params=pltpu.CompilerParams(vmem_limit_bytes=60 * 1024 * 1024),
    )(hidden, norm_gain, box_vec, box_mask, stale_kv)
    far_rows, near_rows = pl.pallas_call(
        weight_body,
        out_shape=(rows(PART), rows(UNIT + HALF - PART)),
        in_specs=[HBM, VM],
        out_specs=(VM, VM),
        scratch_shapes=[pltpu.SemaphoreType.DMA((2,))],
        compiler_params=PARAMS,
    )(weight, begun)
    t3 = lax.ppermute(t3, "patch", x_pairs(1))
    t1 = lax.ppermute(t1, "patch", x_pairs(3))
    near_rows = lax.ppermute(near_rows, "patch", partner_pairs())
    far_rows = lax.ppermute(far_rows, ("dp", "patch"), far_pairs(parts))
    t2a = lax.ppermute(call(pass_back_body, blocks(3), 1)(t1), "patch", x_pairs(3))
    t2b = lax.ppermute(call(pass_on_body, blocks(3), 1)(t3), "patch", x_pairs(1))
    near = call(near_body, blocks(3, 2), 3)(t0, t1, t3)
    near = lax.ppermute(near, "patch", partner_pairs())
    far = call(far_body, blocks(2), 3)(t2a, t2b, near)
    far = lax.ppermute(far, "patch", partner_pairs())

    front, back, opposite, keep = call(
        project_body,
        (blocks(6), blocks(6), blocks(3), blocks(6)),
        8,
        scratch_shapes=[pltpu.VMEM((UNIT, D), BF), pltpu.VMEM((UNIT + HALF, D), BF)],
    )(t0, t1, t2a, t2b, t3, weight, far_rows, near_rows)
    front = lax.ppermute(front, "patch", x_pairs(1))
    back = lax.ppermute(back, "patch", x_pairs(3))
    opposite, mark = lax.optimization_barrier((opposite, back[0, :16, :128]))
    opposite = lax.ppermute(opposite, "patch", x_pairs(2))

    out = call(attend_body, (blocks(5),) + (blocks(),) * 3, 12)(
        keep, front, back, t0, t1, t2a, t2b, t3, near, far, gate, hidden
    )
    fresh, done = call(fresh_body, (jax.ShapeDtypeStruct((1, 2, ROWS, D), BF), MARK), 5)(
        keep, front, back, opposite, mark
    )

    came = {}
    for j in (0, 2, 1, 3):
        pairs = [
            (s * 8 + src, (s + 1) % segments * 8 + dst)
            for s in range(segments)
            for src, dst in x_pairs(j)
        ]
        piece = out[j]
        if j == 0:
            piece, done = lax.optimization_barrier((piece, done))
        came[j] = lax.ppermute(piece, ("segment", "patch"), pairs)
    passed = call(finish_body, jax.ShapeDtypeStruct((1, ROWS, D), BF), 5)(
        came[0], came[3], came[2], came[1], done
    )
    return (passed, fresh)


def solution(mesh):
    placed = (
        P(("dp", "segment"), "patch", None),
        P("segment", None, "patch"),
        P("segment", None),
        P("segment", None),
        P(("dp", "segment"), None),
        P(("dp", "segment"), "patch"),
        P(("dp", "segment"), None, "patch", None),
    )
    return jax.shard_map(
        local,
        mesh=mesh,
        in_specs=placed,
        out_specs=(P(("dp", "segment"), "patch", None), P(("dp", "segment"), None, "patch", None)),
        check_vma=False,
    )
```

```python
import jax
import jax.numpy as jnp
from jax import lax
from jax.experimental import pallas as pl
from jax.experimental.pallas import tpu as pltpu
from jax.sharding import PartitionSpec as P

HEAD_DIM = 128
ROWS = 128
D = 1536
UNIT = 384
HALF = 192
PART = 272
SCALE = HEAD_DIM ** (-0.5) * 1.4426950408889634
BF = jnp.bfloat16
F32 = jnp.float32
MARK = jax.ShapeDtypeStruct((8, 128), F32)
NT = (((1,), (1,)), ((), ()))
VM = pl.BlockSpec(memory_space=pltpu.VMEM)
HBM = pl.BlockSpec(memory_space=pltpu.HBM)
PARAMS = pltpu.CompilerParams(vmem_limit_bytes=16 * 1024 * 1024)


def spot(x, z):
    return 2 * (x % 4) + z


def ahead(z):
    return 1 - 2 * z


def x_pairs(steps):
    return [(spot(x, z), spot(x + ahead(z) * steps, z)) for x in range(4) for z in range(2)]


def partner_pairs():
    return [(spot(x, z), spot(x, 1 - z)) for x in range(4) for z in range(2)]


def far_pairs(parts):
    pairs = []
    for dp in range(parts):
        for x in range(4):
            for z in range(2):
                there = (2 * dp + z - ahead(z)) % (2 * parts)
                pairs.append((dp * 8 + spot(x, z), (there // 2) * 8 + spot(x, there % 2)))
    return pairs


def where_am_i():
    p = lax.axis_index("patch")
    return p // 2, p % 2


def call(body, out, count, **more):
    return pl.pallas_call(
        body,
        out_shape=out,
        in_specs=[VM] * count,
        out_specs=jax.tree.map(lambda _: VM, out),
        compiler_params=PARAMS,
        **more,
    )


def norm_body(h_hbm, g_hbm, b_hbm, m_hbm, s_hbm, own, b1, b2, mark, *scratch):
    mark[...] = jnp.zeros_like(mark)
    h_ref, g_ref, b_ref, m_ref, s_ref, *sems = scratch
    x, z = where_am_i()
    copies = [
        pltpu.make_async_copy(src, dst, sem)
        for src, dst, sem in zip(
            (h_hbm, g_hbm, b_hbm, m_hbm, s_hbm), (h_ref, g_ref, b_ref, m_ref, s_ref), sems
        )
    ]
    for copy in copies:
        copy.start()
    for copy in copies[:4]:
        copy.wait()
    h = h_ref[0].astype(F32)
    inverse = lax.rsqrt(jnp.mean(h * h, axis=-1, keepdims=True) + 1e-06)
    mask = jnp.broadcast_to(m_ref[...].astype(F32), (ROWS, ROWS)).T[:, :1]
    normed = (h * inverse * g_ref[...] + mask * b_ref[...]).astype(BF)
    for bundle in (own, b1, b2):
        for g in range(4):
            bundle[g] = normed[:, UNIT * g : UNIT * (g + 1)]
    copies[4].wait()

    def stale(j, kv):
        group = ((x + (1 - 2 * z) * j + 4) % 4) ^ 1
        return s_ref[0, kv, :, pl.ds(pl.multiple_of(UNIT * group, UNIT), UNIT)]

    for kv in range(2):
        own[4 + kv] = stale(0, kv)
        b1[4 + kv] = stale(1, kv)
        b2[4 + kv] = stale(3, kv)
    b1[6] = stale(2, 0)
    b2[6] = stale(2, 1)


def weight_body(w_hbm, after, far_ref, near_ref, sems):
    del after
    copies = [
        pltpu.make_async_copy(w_hbm.at[:PART], far_ref, sems.at[0]),
        pltpu.make_async_copy(w_hbm.at[PART:], near_ref, sems.at[1]),
    ]
    for copy in copies:
        copy.start()
    for copy in copies:
        copy.wait()


def pass_back_body(t1, o_ref):
    o_ref[0] = t1[0]
    o_ref[1] = t1[1]
    o_ref[2] = t1[6]


def pass_on_body(t3, o_ref):
    o_ref[0] = t3[2]
    o_ref[1] = t3[3]
    o_ref[2] = t3[6]


def near_body(t0, t1, t3, o_ref):
    for i, ref in enumerate((t0, t1, t3)):
        o_ref[i] = ref[4:6]


def far_body(c_ref, d_ref, after, o_ref):
    del after
    o_ref[0] = d_ref[2]
    o_ref[1] = c_ref[2]


def project_body(t0, t1, c_ref, d_ref, t3, w_ref, v_ref, u_ref, early, *outs):
    del early
    front_o, back_o, opp_o, keep_o, both, other = outs
    _, z = where_am_i()
    other[:PART] = v_ref[...]
    other[PART:] = u_ref[...]
    mine = w_ref[pl.ds(pl.multiple_of(UNIT * (1 - z), HALF), HALF), :]
    both[pl.ds(pl.multiple_of(HALF * z, HALF), HALF), :] = mine
    both[pl.ds(pl.multiple_of(HALF * (1 - z), HALF), HALF), :] = other[
        pl.ds(pl.multiple_of(UNIT * z, HALF), HALF), :
    ]
    placed = [[t[g] for g in range(4)] for t in (t0, t1, t3)]
    placed.insert(2, [c_ref[0], c_ref[1], d_ref[0], d_ref[1]])
    tokens = jnp.concatenate([jnp.concatenate(b, axis=1) for b in placed], axis=0)

    def product(weight):
        got = lax.dot_general(tokens, weight, NT, preferred_element_type=F32).astype(BF)
        return [got[ROWS * j : ROWS * (j + 1)] for j in range(4)]

    front = product(w_ref[pl.ds(pl.multiple_of(HALF * z, HALF), UNIT), :])
    mid = product(both[...])
    back = product(other[pl.ds(pl.multiple_of(HALF * (1 - z), HALF), UNIT), :])
    for j in range(4):
        front_o[j] = front[j]
        back_o[j] = back[j]
        keep_o[j] = mid[j]
    front_o[4] = mid[1]
    front_o[5] = back[1]
    back_o[4] = mid[3]
    back_o[5] = front[3]
    opp_o[0] = front[2]
    opp_o[1] = mid[2]
    opp_o[2] = back[2]
    keep_o[4] = front[0]
    keep_o[5] = back[0]


def roles(x, z):
    left = 1 + z
    right = 2 - z
    q = jnp.where(x == 0, 0, jnp.where(x == 3, right, left))
    k = jnp.where(x == 0, right, jnp.where(x == 3, left, 0))
    v = jnp.where(x == 0, left, jnp.where(x == 3, 0, right))
    return q, k, v


def attend_body(m_ref, a_ref, b_ref, t0, t1, c_ref, d_ref, t3, pn_ref, pf_ref, g_ref, *o_refs):
    x, z = where_am_i()
    gates = g_ref[:, pl.ds(pl.multiple_of(UNIT * (x ^ 1), UNIT), UNIT)]
    roled = roles(x, z)
    units = [(head, j) for head in range(3) for j in range(4)]

    def part(index, j, cols):
        own = m_ref[j, :, cols]
        behind = a_ref[(j + 1) % 4, :, cols]
        ahead = b_ref[(j + 3) % 4, :, cols]
        return jnp.where(index == 0, own, jnp.where(index == 1, behind, ahead))

    def used(kv, j, cols):
        blocks = [t0[4 + kv, :, cols], t1[4 + kv, :, cols]]
        blocks += [(d_ref, c_ref)[kv][2, :, cols], t3[4 + kv, :, cols]]
        blocks += [pn_ref[i, kv, :, cols] for i in range(3)]
        blocks += [pf_ref[kv, :, cols]]
        blocks[j] = part(roled[1 + kv], j, cols)
        return jnp.concatenate(blocks, axis=0)

    def columns(head):
        return slice(HEAD_DIM * head, HEAD_DIM * (head + 1))

    def score(head, j):
        cols = columns(head)
        return lax.dot_general(
            part(roled[0], j, cols), used(0, j, cols), NT, preferred_element_type=F32
        )

    def finish(head, j, weights, total):
        cols = columns(head)
        summed = jnp.dot(weights, used(1, j, cols), preferred_element_type=F32)
        o_refs[j][:, cols] = (gates[:, cols] * (summed * (1.0 / total))).astype(BF)

    coming = score(*units[0])
    behind = None
    for n, unit in enumerate(units):
        scores = coming * SCALE
        if n + 1 < len(units):
            coming = score(*units[n + 1])
        if behind is not None:
            finish(*behind)
        top = jnp.max(scores, axis=-1, keepdims=True)
        weights = jnp.exp2(scores - top)
        behind = (*unit, weights.astype(BF), jnp.sum(weights, axis=-1, keepdims=True))
    finish(*behind)


def fresh_body(k_ref, a_ref, b_ref, p_ref, after, f_ref, mark):
    del after
    mark[...] = jnp.zeros_like(mark)
    x, z = where_am_i()
    rows = (
        (0, (k_ref.at[4], k_ref.at[0], k_ref.at[5])),
        (1, (b_ref.at[5], b_ref.at[4], b_ref.at[3])),
        (2, (p_ref.at[0], p_ref.at[1], p_ref.at[2])),
        (3, (a_ref.at[1], a_ref.at[4], a_ref.at[5])),
    )
    for j, refs in rows:
        source = (x + (1 - 2 * z) * j + 4) % 4
        for unit, ref in zip((2 * z, 1, 2 - 2 * z), refs):
            g = 3 * source + unit

            @pl.when(g >= 4)
            def _():
                cols = pl.ds(pl.multiple_of(UNIT * (g % 4), UNIT), UNIT)
                f_ref[0, g // 4 - 1, :, cols] = ref[...]


def finish_body(a0, a1, a2, a3, h_ref, after, o_ref):
    del after
    x, z = where_am_i()
    for j, ref in enumerate((a0, a1, a2, a3)):
        group = ((x + (1 - 2 * z) * j + 4) % 4) ^ 1
        cols = pl.ds(pl.multiple_of(UNIT * group, UNIT), UNIT)
        o_ref[0, :, cols] = (h_ref[0, :, cols].astype(F32) + ref[...].astype(F32)).astype(BF)


def local(hidden, w_qkv, norm_gain, box_vec, gate, box_mask, stale_kv):
    parts = lax.axis_size("dp")
    segments = lax.axis_size("segment")

    def blocks(*lead):
        return jax.ShapeDtypeStruct((*lead, ROWS, UNIT), BF)

    def rows(count):
        return jax.ShapeDtypeStruct((count, D), BF)

    weight = jnp.swapaxes(w_qkv[0], 0, 1)
    t0, t3, t1, begun = pl.pallas_call(
        norm_body,
        out_shape=(blocks(6), blocks(7), blocks(7), MARK),
        in_specs=[HBM] * 5,
        out_specs=(VM,) * 4,
        scratch_shapes=[
            pltpu.VMEM((1, ROWS, D), BF),
            pltpu.VMEM((1, D), F32),
            pltpu.VMEM((1, D), F32),
            pltpu.VMEM((1, ROWS), jnp.int32),
            pltpu.VMEM((1, 2, ROWS, D), BF),
        ]
        + [pltpu.SemaphoreType.DMA] * 5,
        compiler_params=pltpu.CompilerParams(vmem_limit_bytes=60 * 1024 * 1024),
    )(hidden, norm_gain, box_vec, box_mask, stale_kv)
    far_rows, near_rows = pl.pallas_call(
        weight_body,
        out_shape=(rows(PART), rows(UNIT + HALF - PART)),
        in_specs=[HBM, VM],
        out_specs=(VM, VM),
        scratch_shapes=[pltpu.SemaphoreType.DMA((2,))],
        compiler_params=PARAMS,
    )(weight, begun)
    t3 = lax.ppermute(t3, "patch", x_pairs(1))
    t1 = lax.ppermute(t1, "patch", x_pairs(3))
    near_rows = lax.ppermute(near_rows, "patch", partner_pairs())
    far_rows = lax.ppermute(far_rows, ("dp", "patch"), far_pairs(parts))
    before = lax.ppermute(hidden, "segment", [(i, (i + 1) % segments) for i in range(segments)])

    t2a = lax.ppermute(call(pass_back_body, blocks(3), 1)(t1), "patch", x_pairs(3))
    t2b = lax.ppermute(call(pass_on_body, blocks(3), 1)(t3), "patch", x_pairs(1))
    near = call(near_body, blocks(3, 2), 3)(t0, t1, t3)
    near = lax.ppermute(near, "patch", partner_pairs())
    far = call(far_body, blocks(2), 3)(t2a, t2b, near)
    far = lax.ppermute(far, "patch", partner_pairs())

    front, back, opposite, keep = call(
        project_body,
        (blocks(6), blocks(6), blocks(3), blocks(6)),
        9,
        scratch_shapes=[pltpu.VMEM((UNIT, D), BF), pltpu.VMEM((UNIT + HALF, D), BF)],
    )(t0, t1, t2a, t2b, t3, weight, far_rows, near_rows, before)
    front = lax.ppermute(front, "patch", x_pairs(1))
    back = lax.ppermute(back, "patch", x_pairs(3))
    opposite, mark = lax.optimization_barrier((opposite, back[0, :16, :128]))
    opposite = lax.ppermute(opposite, "patch", x_pairs(2))

    out = call(attend_body, (blocks(),) * 4, 11)(
        keep, front, back, t0, t1, t2a, t2b, t3, near, far, gate
    )
    fresh, done = call(fresh_body, (jax.ShapeDtypeStruct((1, 2, ROWS, D), BF), MARK), 5)(
        keep, front, back, opposite, mark
    )

    came = {}
    for j in (2, 1, 3, 0):
        pairs = [
            (s * 8 + src, (s + 1) % segments * 8 + dst)
            for s in range(segments)
            for src, dst in x_pairs(j)
        ]
        came[j] = lax.ppermute(out[j], ("segment", "patch"), pairs)
    passed = call(finish_body, jax.ShapeDtypeStruct((1, ROWS, D), BF), 6)(
        came[0], came[3], came[2], came[1], before, done
    )
    return (passed, fresh)


def solution(mesh):
    placed = (
        P(("dp", "segment"), "patch", None),
        P("segment", None, "patch"),
        P("segment", None),
        P("segment", None),
        P(("dp", "segment"), None),
        P(("dp", "segment"), "patch"),
        P(("dp", "segment"), None, "patch", None),
    )
    return jax.shard_map(
        local,
        mesh=mesh,
        in_specs=placed,
        out_specs=(P(("dp", "segment"), "patch", None), P(("dp", "segment"), None, "patch", None)),
        check_vma=False,
    )
```
